32 devices in a mesh: dp: 8 (over y, x, core), mp: 4 (over z).
Axes of the slice: x: 2, y: 2, z: 4, core: 2. Of those that a mesh axis runs over, the one named last changes fastest.
Arguments:
- tokens: bfloat16 [8192, 1024], P(('dp', 'mp')), may hold values from -6 to 6
- cotangent: bfloat16 [8192, 1024], P(('dp', 'mp')), may hold values from -6 to 6
- weight_in: float32 [1024, 4096], P('dp', 'mp'), may hold values from -0.1875 to 0.1875
- weight_out: float32 [4096, 1024], P('mp', 'dp'), may hold values from -0.09375 to 0.09375
- moment_in: float32 [1024, 4096], P('dp', 'mp'), may hold values from -4 to 4
- second_in: float32 [1024, 4096], P('dp', 'mp'), may hold values from 0.01 to 1
- moment_out: float32 [4096, 1024], P('mp', 'dp'), may hold values from -4 to 4
- second_out: float32 [4096, 1024], P('mp', 'dp'), may hold values from 0.01 to 1
Outputs:
- input_grad: bfloat16 [8192, 1024], P(('dp', 'mp'))
- new_weight_in: float32 [1024, 4096], P('dp', 'mp')
- new_moment_in: float32 [1024, 4096], P('dp', 'mp')
- new_second_in: float32 [1024, 4096], P('dp', 'mp')
- new_weight_out: float32 [4096, 1024], P('mp', 'dp')
- new_moment_out: float32 [4096, 1024], P('mp', 'dp')
- new_second_out: float32 [4096, 1024], P('mp', 'dp')
The draws below stay inside these ranges and needn't reach their ends.
All inputs are finite; a program needn't handle non-finite values.
Results may differ from the reference program's by a relative error of at most 0.0071.
Values may be sent and summed in bfloat16 or wider, within the bound.
A program may use at most 64 MiB of HBM per device.

```python
import math
import jax
import jax.numpy as jnp
from jax import lax

D = 1024
FF = 4096
TOK_DEV = 256
STEP = 1000
TOKENS = 8192
N_MP = 4


def raised(entries, key, source, target, parts, factor):
    owner, partner = [(jnp.arange(entries.shape[position]) // (entries.shape[position] // parts)).reshape([-1 if axis == position else 1 for axis in range(entries.ndim)]) for position in (source, target)]
    chosen = jax.random.permutation(key, parts)[partner]
    strong = (owner == chosen) | (owner == (partner + parts // 2) % parts)
    return jnp.where(strong, factor * entries, entries)


def levels(own_key, dims, shards, smallest, largest):
    factor_of = 1.0
    for axis_at, shards_of in shards:
        draws = jax.random.uniform(jax.random.fold_in(jax.random.fold_in(own_key, 6), axis_at), (shards_of,), jnp.float32, smallest / len(shards), largest / len(shards))
        factor_of = factor_of * jnp.repeat(jnp.exp(draws), dims[axis_at] // shards_of).reshape((-1,) + (1,) * (len(dims) - 1 - axis_at))
    return factor_of


def bell_draw(stream_key, extent, spread, reach, cuts=(), held_as=jnp.bfloat16):
    entries = spread * jax.random.normal(stream_key, extent, jnp.float32)
    if cuts:
        entries = entries * levels(stream_key, extent, cuts, -0.22, 0.18)
    return jnp.clip(entries, -reach, reach).astype(held_as)


def heavy_noise(stream_key, dims, deviation, bound, pieces, heavy, held_as=jnp.bfloat16):
    array = deviation * jax.random.normal(stream_key, dims, jnp.float32)
    if pieces:
        array = array * levels(stream_key, dims, pieces, -0.22, 0.18)
    return jnp.clip(raised(array, jax.random.fold_in(stream_key, 3), *heavy), -bound, bound).astype(held_as)


def setup_inputs(seed: int = 0) -> dict:
    streams_of = jax.random.split(jax.random.key(seed), 9)
    tokens = bell_draw(streams_of[0], (TOKENS, D), 1.0, 6.0, ((0, 32),))
    cotangent = heavy_noise(streams_of[1], (TOKENS, D), 1.0, 6.0, ((0, 32),), (0, 1, 32, 2.75))
    weight_in = bell_draw(streams_of[2], (D, FF), D ** -0.5, 0.1875, ((0, 8), (1, 4)), jnp.float32)
    weight_out = bell_draw(streams_of[3], (FF, D), FF ** -0.5, 0.09375, ((0, 4), (1, 8)), jnp.float32)
    moment_in = bell_draw(streams_of[4], (D, FF), 0.3, 4.0, ((0, 8), (1, 4)), jnp.float32)
    second_in = jnp.clip(jnp.exp(math.log(1.0) - 4.6051702 * jax.random.uniform(streams_of[5], (D, FF), jnp.float32) ** levels(streams_of[5], (D, FF), ((0, 8), (1, 4)), -0.2, 0.2)), 0.01, 1.0)
    moment_out = bell_draw(streams_of[6], (FF, D), 0.3, 4.0, ((0, 4), (1, 8)), jnp.float32)
    second_out = jnp.clip(jnp.exp(math.log(1.0) - 4.6051702 * jax.random.uniform(streams_of[7], (FF, D), jnp.float32) ** levels(streams_of[7], (FF, D), ((0, 4), (1, 8)), -0.2, 0.2)), 0.01, 1.0)
    return {"tokens": tokens, "cotangent": cotangent, "weight_in": weight_in, "weight_out": weight_out, "moment_in": moment_in, "second_in": second_in, "moment_out": moment_out, "second_out": second_out}


BETA_ONE = 0.9
BETA_TWO = 0.999
EPSILON = 1e-08
LEARN_RATE = 0.001
DECAY_RATE = 0.1

def normalize(rows):
    values = rows.astype(jnp.float32)
    inverse = lax.rsqrt(lax.optimization_barrier(jnp.mean(values * values, axis=-1, keepdims=True)) + 1e-06)
    return (values * inverse, inverse)

def activate(values):
    return jax.nn.gelu(values, approximate=True)

def adam_step(weight, moment, second, gradient):
    moment_new = BETA_ONE * moment + (1.0 - BETA_ONE) * gradient
    second_new = BETA_TWO * second + (1.0 - BETA_TWO) * gradient * gradient
    first_fix = 1.0 - BETA_ONE ** float(STEP)
    second_fix = 1.0 - BETA_TWO ** float(STEP)
    update = moment_new / first_fix / (jnp.sqrt(second_new / second_fix) + EPSILON)
    weight_new = weight - LEARN_RATE * (update + DECAY_RATE * weight)
    return (weight_new, moment_new, second_new)

def contract_rows(left, right):
    return lax.dot_general(left, right, (((0,), (0,)), ((), ())), preferred_element_type=jnp.float32)

def reference(tokens, cotangent, weight_in, weight_out, moment_in, second_in, moment_out, second_out):
    weight_in_b = weight_in.astype(jnp.bfloat16)
    weight_out_b = weight_out.astype(jnp.bfloat16)
    block = TOK_DEV * N_MP
    token_blocks = tokens.reshape(TOKENS // block, block, D)
    grad_blocks = cotangent.reshape(TOKENS // block, block, D)

    def visit(carry, pair):
        rows, upstream = pair
        normed_f, inverse = normalize(rows)
        normed = normed_f.astype(jnp.bfloat16)
        preact = jnp.dot(normed, weight_in_b, preferred_element_type=jnp.float32)
        activated, backward = jax.vjp(activate, preact)
        hidden = activated.astype(jnp.bfloat16)
        grad_out = carry[1] + contract_rows(hidden, upstream)
        d_hidden = lax.dot_general(upstream, weight_out_b, (((1,), (1,)), ((), ())), preferred_element_type=jnp.float32)
        d_preact = backward(d_hidden)[0].astype(jnp.bfloat16)
        grad_in = carry[0] + contract_rows(normed, d_preact)
        d_normed = lax.dot_general(d_preact, weight_in_b, (((1,), (1,)), ((), ())), preferred_element_type=jnp.float32)
        d_rows = inverse * (d_normed - normed_f * lax.optimization_barrier(jnp.mean(d_normed * normed_f, axis=-1, keepdims=True)))
        return ((grad_in, grad_out), d_rows.astype(jnp.bfloat16))
    start = (jnp.zeros((D, FF), jnp.float32), jnp.zeros((FF, D), jnp.float32))
    sums, input_blocks = lax.scan(visit, start, (token_blocks, grad_blocks))
    grad_scale = 1.0 / jnp.sqrt(jnp.float32(TOKENS))
    grad_in = sums[0] * grad_scale
    grad_out = sums[1] * grad_scale
    new_weight_in, new_moment_in, new_second_in = adam_step(weight_in, moment_in, second_in, grad_in)
    new_weight_out, new_moment_out, new_second_out = adam_step(weight_out, moment_out, second_out, grad_out)
    input_grad = input_blocks.reshape(TOKENS, D)
    return (input_grad, new_weight_in, new_moment_in, new_second_in, new_weight_out, new_moment_out, new_second_out)
```

```python
import functools
import math

import jax
import jax.numpy as jnp
from jax import lax
from jax.experimental import pallas as pl
from jax.experimental.pallas import tpu as pltpu
from jax.sharding import PartitionSpec as P

MESH = pl.DeviceIdType.MESH
STEP = 1000

BETA_ONE = 0.9
BETA_TWO = 0.999
EPSILON = 1e-08
LEARN_RATE = 0.001
DECAY_RATE = 0.1
CUBIC = 0.044715
ROOT = math.sqrt(2.0 / math.pi)


def adam_step(weight, moment, second, gradient):
    moment_new = BETA_ONE * moment + (1.0 - BETA_ONE) * gradient
    second_new = BETA_TWO * second + (1.0 - BETA_TWO) * gradient * gradient
    first_fix = 1.0 - BETA_ONE ** float(STEP)
    second_fix = 1.0 - BETA_TWO ** float(STEP)
    update = moment_new / first_fix / (jnp.sqrt(second_new / second_fix) + EPSILON)
    weight_new = weight - LEARN_RATE * (update + DECAY_RATE * weight)
    return (weight_new, moment_new, second_new)


def gelu_pair(v):
    square = v * v
    t = jnp.tanh(ROOT * (v + CUBIC * (square * v)))
    half = 0.5 * (1.0 + t)
    slope = half + (0.5 * ROOT) * v * (1.0 - t * t) * (1.0 + (3.0 * CUBIC) * square)
    return v * half, slope


def kernel(
    n_dp, n_mp, tile,
    tokens_ref, cot_ref, win_ref, wout_ref,
    ig_ref, gin_ref, gout_ref,
    held, weights, grads, flipped, dn, ret_out, ret_in, sib_out, sib_in, chip_out, chip_in,
    tok_send, tok_recv, w_send, w_sib, w_recv, ret_send, ret_recv, sib_send, sib_recv, chip_send, chip_recv,
):
    n_chip = n_dp // 2
    dp, z = lax.axis_index("dp"), lax.axis_index("mp")
    chip, core = dp // 2, dp % 2
    sibling = chip * 2 + (1 - core)
    rows = win_ref.shape[0]
    hidden_units = win_ref.shape[1]
    f32, b16 = jnp.float32, jnp.bfloat16

    def other_chip(i):
        return (chip + i) % n_chip

    barrier = pltpu.get_barrier_semaphore()
    pl.semaphore_signal(barrier, inc=1, device_id=(sibling, z), device_id_type=MESH)
    for i in range(1, n_chip):
        pl.semaphore_signal(barrier, inc=1, device_id=(other_chip(i) * 2 + core, z), device_id_type=MESH)
    for i in range(1, n_mp):
        pl.semaphore_signal(barrier, inc=1, device_id=(dp, (z + i) % n_mp), device_id_type=MESH)

    values = tokens_ref[...].astype(f32)
    inverse = lax.rsqrt(jnp.mean(values * values, axis=-1, keepdims=True) + 1e-06)
    held[z, 0] = (values * inverse).astype(b16)
    held[z, 1] = cot_ref[...]
    own_rows = pl.ds(pl.multiple_of(dp * rows, rows), rows)
    weights[0, own_rows, :] = win_ref[...].astype(b16)
    weights[1, own_rows, :] = wout_ref[...].T.astype(b16)
    pl.semaphore_wait(barrier, n_chip + n_mp - 1)

    def tok_copy(origin, side, target):
        return pltpu.make_async_remote_copy(
            src_ref=held.at[origin], dst_ref=held.at[origin],
            send_sem=tok_send.at[side, origin], recv_sem=tok_recv.at[origin],
            device_id=(dp, target), device_id_type=MESH)

    def weight_copy(owner, send_sem, target):
        block = weights.at[:, pl.ds(pl.multiple_of(owner * rows, rows), rows), :]
        return pltpu.make_async_remote_copy(
            src_ref=block, dst_ref=block, send_sem=send_sem, recv_sem=w_recv.at[owner],
            device_id=(target, z), device_id_type=MESH)

    def ret_copy(origin):
        return pltpu.make_async_remote_copy(
            src_ref=ret_out.at[origin], dst_ref=ret_in.at[z],
            send_sem=ret_send.at[origin], recv_sem=ret_recv.at[z],
            device_id=(dp, origin), device_id_type=MESH)

    def ret_arrival(sender):
        return pltpu.make_async_remote_copy(
            src_ref=ret_in.at[sender], dst_ref=ret_in.at[sender],
            send_sem=ret_send.at[sender], recv_sem=ret_recv.at[sender],
            device_id=(dp, sender), device_id_type=MESH)

    def sib_copy(k):
        return pltpu.make_async_remote_copy(
            src_ref=sib_out.at[k], dst_ref=sib_in.at[k],
            send_sem=sib_send.at[k], recv_sem=sib_recv.at[k],
            device_id=(sibling, z), device_id_type=MESH)

    def chip_copy(k):
        return pltpu.make_async_remote_copy(
            src_ref=chip_out.at[k], dst_ref=chip_in.at[chip],
            send_sem=chip_send.at[k], recv_sem=chip_recv.at[chip],
            device_id=(k * 2 + core, z), device_id_type=MESH)

    def chip_arrival(k):
        return pltpu.make_async_remote_copy(
            src_ref=chip_in.at[k], dst_ref=chip_in.at[k],
            send_sem=chip_send.at[k], recv_sem=chip_recv.at[k],
            device_id=(k * 2 + core, z), device_id_type=MESH)

    @pl.when(z < n_mp - 1)
    def _():
        tok_copy(z, 0, z + 1).start()

    @pl.when(z > 0)
    def _():
        tok_copy(z, 1, z - 1).start()

    for i in range(1, n_chip):
        k = other_chip(i)
        weight_copy(dp, w_send.at[k], k * 2 + core).start()
    weight_copy(dp, w_sib.at[chip], sibling).start()

    def clear(i, carry):
        part = pl.ds(pl.multiple_of(i * rows, rows), rows)
        grads[:, part, :] = jnp.zeros((2, rows, hidden_units), f32)
        return carry

    lax.fori_loop(0, n_dp, clear, 0)

    for i in range(1, n_chip):
        owner = other_chip(i) * 2 + core
        weight_copy(owner, w_sib.at[other_chip(i)], sibling).wait_recv()
        weight_copy(owner, w_sib.at[other_chip(i)], sibling).start()

    def pass_on(distance):
        @pl.when(z - distance >= 0)
        def _():
            tok_copy(z - distance, 0, z).wait_recv()

            @pl.when(z < n_mp - 1)
            def _():
                tok_copy(z - distance, 0, z + 1).start()

        @pl.when(z + distance < n_mp)
        def _():
            tok_copy(z + distance, 1, z).wait_recv()

            @pl.when(z > 0)
            def _():
                tok_copy(z + distance, 1, z - 1).start()

    pass_on(1)
    for k in range(n_chip):
        weight_copy(k * 2 + (1 - core), w_sib.at[k], sibling).wait_recv()

    at_end = (z == 0) | (z == n_mp - 1)

    def chunk(origin):
        flipped[0] = held[origin, 0].T
        flipped[1] = held[origin, 1].T

        def columns(step, carry):
            part = pl.ds(pl.multiple_of(step * tile, tile), tile)
            w_in = weights[0, :, part]
            preact = jnp.dot(held[origin, 0], w_in, preferred_element_type=f32)
            d_hidden = jnp.dot(held[origin, 1], weights[1, :, part], preferred_element_type=f32)
            hidden, slope = gelu_pair(preact)
            d_preact = (d_hidden * slope).astype(b16)
            grads[0, :, part] += jnp.dot(flipped[0], d_preact, preferred_element_type=f32)
            grads[1, :, part] += jnp.dot(flipped[1], hidden.astype(b16), preferred_element_type=f32)
            back = lax.dot_general(d_preact, w_in, (((1,), (1,)), ((), ())), preferred_element_type=f32)

            @pl.when(step == 0)
            def _():
                dn[...] = back

            @pl.when(step > 0)
            def _():
                dn[...] += back
            return carry

        lax.fori_loop(0, hidden_units // tile, columns, 0)

        @pl.when(origin == z)
        def _():
            ig_ref[...] = dn[...]

        @pl.when(origin != z)
        def _():
            ret_out[origin] = dn[...].astype(b16)

            @pl.when(at_end)
            def _():
                ret_copy(origin).start()

    def at_distance(distance, carry):
        @pl.when(distance >= 2)
        def _():
            pass_on(distance)

        def side(which, inner):
            origin = z + distance * (2 * which - 1)

            @pl.when((origin >= 0) & (origin < n_mp) & (distance + which > 0))
            def _():
                chunk(jnp.where(distance == 0, z, origin))
            return inner

        lax.fori_loop(jnp.where(distance == 0, 1, 0), 2, side, 0)
        return carry

    lax.fori_loop(0, n_mp, at_distance, 0)

    def block(owner):
        return grads[:, pl.ds(pl.multiple_of(owner * rows, rows), rows), :]

    for i in range(n_chip):
        k = other_chip(i + 1)
        sib_out[k] = block(k * 2 + (1 - core)).astype(b16)
        sib_copy(k).start()
    for i in range(1, n_chip):
        k = other_chip(i)
        sib_copy(k).wait_recv()
        chip_out[k] = (block(k * 2 + core) + sib_in[k].astype(f32)).astype(b16)
        chip_copy(k).start()

    for origin in range(n_mp):
        @pl.when((z < n_mp - 1) & (origin <= z))
        def _():
            tok_copy(origin, 0, z + 1).wait_send()

        @pl.when((z > 0) & (origin >= z))
        def _():
            tok_copy(origin, 1, z - 1).wait_send()
    for origin in range(n_mp):
        @pl.when((origin != z) & jnp.logical_not(at_end))
        def _():
            ret_copy(origin).start()

    sib_copy(chip).wait_recv()
    total = block(dp) + sib_in[chip].astype(f32)
    for i in range(1, n_chip):
        k = other_chip(i)
        chip_arrival(k).wait_recv()
        total += chip_in[k].astype(f32)
    gin_ref[...] = total[0]
    gout_ref[...] = total[1].T

    for i in range(1, n_mp):
        sender = (z + i) % n_mp
        ret_arrival(sender).wait_recv()
        ig_ref[...] += ret_in[sender].astype(f32)
    values = tokens_ref[...].astype(f32)
    inverse = lax.rsqrt(jnp.mean(values * values, axis=-1, keepdims=True) + 1e-06)
    normed = values * inverse
    d_normed = ig_ref[...]
    ig_ref[...] = inverse * (d_normed - normed * jnp.mean(d_normed * normed, axis=-1, keepdims=True))

    for i in range(1, n_chip):
        k = other_chip(i)
        weight_copy(dp, w_send.at[k], k * 2 + core).wait_send()
        chip_copy(k).wait_send()
    for k in range(n_chip):
        weight_copy(k * 2 + core, w_sib.at[k], sibling).wait_send()
        sib_copy(k).wait_send()
    for i in range(1, n_mp):
        ret_copy((z + i) % n_mp).wait_send()


def shards(n_dp, n_mp, tokens, cotangent, weight_in, weight_out, moment_in, second_in, moment_out, second_out):
    count, width = tokens.shape
    rows, units = weight_in.shape
    n_chip = n_dp // 2
    b16, f32 = jnp.bfloat16, jnp.float32
    vmem = pl.BlockSpec(memory_space=pltpu.VMEM)
    dma = pltpu.SemaphoreType.DMA
    flops = 10 * count * n_mp * width * units
    d_rows, grad_in, grad_out = pl.pallas_call(
        functools.partial(kernel, n_dp, n_mp, min(256, units)),
        out_shape=(
            jax.ShapeDtypeStruct((count, width), f32),
            jax.ShapeDtypeStruct((rows, units), f32),
            jax.ShapeDtypeStruct((units, rows), f32),
        ),
        in_specs=[vmem] * 4,
        out_specs=(vmem,) * 3,
        scratch_shapes=[
            pltpu.VMEM((n_mp, 2, count, width), b16),
            pltpu.VMEM((2, width, units), b16),
            pltpu.VMEM((2, width, units), f32),
            pltpu.VMEM((2, width, count), b16),
            pltpu.VMEM((count, width), f32),
            pltpu.VMEM((n_mp, count, width), b16),
            pltpu.VMEM((n_mp, count, width), b16),
            pltpu.VMEM((n_chip, 2, rows, units), b16),
            pltpu.VMEM((n_chip, 2, rows, units), b16),
            pltpu.VMEM((n_chip, 2, rows, units), b16),
            pltpu.VMEM((n_chip, 2, rows, units), b16),
            dma((2, n_mp)), dma((n_mp,)),
            dma((n_chip,)), dma((n_chip,)), dma((n_dp,)),
            dma((n_mp,)), dma((n_mp,)),
            dma((n_chip,)), dma((n_chip,)),
            dma((n_chip,)), dma((n_chip,)),
        ],
        compiler_params=pltpu.CompilerParams(
            collective_id=0, has_side_effects=True, vmem_limit_bytes=56 * 1024 * 1024
        ),
        cost_estimate=pl.CostEstimate(flops=flops, bytes_accessed=8 * rows * units * 4, transcendentals=0),
    )(tokens, cotangent, weight_in, weight_out)
    input_grad = d_rows.astype(b16)
    grad_scale = 1.0 / jnp.sqrt(jnp.float32(count * n_dp * n_mp))
    new_in = adam_step(weight_in, moment_in, second_in, grad_in * grad_scale)
    new_out = adam_step(weight_out, moment_out, second_out, grad_out * grad_scale)
    return (input_grad, *new_in, *new_out)


def solution(mesh):
    return jax.shard_map(
        functools.partial(shards, mesh.shape["dp"], mesh.shape["mp"]),
        mesh=mesh,
        in_specs=(
            P(("dp", "mp"), None),
            P(("dp", "mp"), None),
            P("dp", "mp"),
            P("mp", "dp"),
            P("dp", "mp"),
            P("dp", "mp"),
            P("mp", "dp"),
            P("mp", "dp"),
        ),
        out_specs=(
            P(("dp", "mp"), None),
            P("dp", "mp"),
            P("dp", "mp"),
            P("dp", "mp"),
            P("mp", "dp"),
            P("mp", "dp"),
            P("mp", "dp"),
        ),
        check_vma=False,
    )
```

```python
import functools
import math

import jax
import jax.numpy as jnp
from jax import lax
from jax.experimental import pallas as pl
from jax.experimental.pallas import tpu as pltpu
from jax.sharding import PartitionSpec as P

MESH = pl.DeviceIdType.MESH
STEP = 1000

BETA_ONE = 0.9
BETA_TWO = 0.999
EPSILON = 1e-08
LEARN_RATE = 0.001
DECAY_RATE = 0.1
CUBIC = 0.044715
ROOT = math.sqrt(2.0 / math.pi)


def adam_step(weight, moment, second, gradient):
    moment_new = BETA_ONE * moment + (1.0 - BETA_ONE) * gradient
    second_new = BETA_TWO * second + (1.0 - BETA_TWO) * gradient * gradient
    first_fix = 1.0 - BETA_ONE ** float(STEP)
    second_fix = 1.0 - BETA_TWO ** float(STEP)
    update = moment_new / first_fix / (jnp.sqrt(second_new / second_fix) + EPSILON)
    weight_new = weight - LEARN_RATE * (update + DECAY_RATE * weight)
    return (weight_new, moment_new, second_new)


def gelu_pair(v):
    square = v * v
    t = jnp.tanh(ROOT * (v + CUBIC * (square * v)))
    half = 0.5 * (1.0 + t)
    slope = half + (0.5 * ROOT) * v * (1.0 - t * t) * (1.0 + (3.0 * CUBIC) * square)
    return v * half, slope


def kernel(
    n_dp, n_mp, tile,
    tokens_ref, cot_ref, win_ref, wout_ref,
    ig_ref, gin_ref, gout_ref,
    held, weights, grads, flipped, dn, own, ret_out, ret_in, sib_out, sib_in, chip_out, chip_in,
    tok_send, tok_recv, w_send, w_sib, w_recv, ret_send, ret_recv, sib_send, sib_recv, chip_send, chip_recv,
):
    n_chip = n_dp // 2
    dp, z = lax.axis_index("dp"), lax.axis_index("mp")
    chip, core = dp // 2, dp % 2
    sibling = chip * 2 + (1 - core)
    rows = win_ref.shape[0]
    hidden_units = win_ref.shape[1]
    f32, b16 = jnp.float32, jnp.bfloat16
    n_tile = hidden_units // tile
    n_ret = ret_send.shape[1]
    ret_rows = tokens_ref.shape[0] // n_ret

    def other_chip(i):
        return (chip + i) % n_chip

    barrier = pltpu.get_barrier_semaphore()
    pl.semaphore_signal(barrier, inc=1, device_id=(sibling, z), device_id_type=MESH)
    for i in range(1, n_chip):
        pl.semaphore_signal(barrier, inc=1, device_id=(other_chip(i) * 2 + core, z), device_id_type=MESH)
    for i in range(1, n_mp):
        pl.semaphore_signal(barrier, inc=1, device_id=(dp, (z + i) % n_mp), device_id_type=MESH)

    values = tokens_ref[...].astype(f32)
    inverse = lax.rsqrt(jnp.mean(values * values, axis=-1, keepdims=True) + 1e-06)
    held[z, 0] = (values * inverse).astype(b16)
    held[z, 1] = cot_ref[...]
    own_rows = pl.ds(pl.multiple_of(dp * rows, rows), rows)
    weights[0, own_rows, :] = win_ref[...].astype(b16)
    weights[1, own_rows, :] = wout_ref[...].T.astype(b16)
    pl.semaphore_wait(barrier, n_chip + n_mp - 1)

    def tok_copy(origin, piece, side, target):
        return pltpu.make_async_remote_copy(
            src_ref=held.at[origin, piece], dst_ref=held.at[origin, piece],
            send_sem=tok_send.at[side, origin, piece], recv_sem=tok_recv.at[origin, piece],
            device_id=(dp, target), device_id_type=MESH)

    def weight_copy(owner, send_sem, target):
        block = weights.at[:, pl.ds(pl.multiple_of(owner * rows, rows), rows), :]
        return pltpu.make_async_remote_copy(
            src_ref=block, dst_ref=block, send_sem=send_sem, recv_sem=w_recv.at[owner],
            device_id=(target, z), device_id_type=MESH)

    def ret_copy(target, step, way):
        part = pl.ds(step * ret_rows, ret_rows)
        slot = jnp.where((z + way == target) & (way == 1), n_mp, target)
        return pltpu.make_async_remote_copy(
            src_ref=ret_out.at[target, part], dst_ref=ret_in.at[slot, part],
            send_sem=ret_send.at[target, step], recv_sem=ret_recv.at[slot, step],
            device_id=(dp, z + way), device_id_type=MESH)

    def ret_arrival(slot, step):
        part = pl.ds(step * ret_rows, ret_rows)
        return pltpu.make_async_remote_copy(
            src_ref=ret_in.at[slot, part], dst_ref=ret_in.at[slot, part],
            send_sem=ret_send.at[0, step], recv_sem=ret_recv.at[slot, step],
            device_id=(dp, z), device_id_type=MESH)

    def sib_copy(t):
        return pltpu.make_async_remote_copy(
            src_ref=sib_out.at[t], dst_ref=sib_in.at[t],
            send_sem=sib_send.at[t], recv_sem=sib_recv.at[t],
            device_id=(sibling, z), device_id_type=MESH)

    def chip_copy(t, k):
        return pltpu.make_async_remote_copy(
            src_ref=chip_out.at[t, k], dst_ref=chip_in.at[t, chip],
            send_sem=chip_send.at[t, k], recv_sem=chip_recv.at[t, chip],
            device_id=(k * 2 + core, z), device_id_type=MESH)

    def chip_arrival(t, k):
        return pltpu.make_async_remote_copy(
            src_ref=chip_in.at[t, k], dst_ref=chip_in.at[t, k],
            send_sem=chip_send.at[t, k], recv_sem=chip_recv.at[t, k],
            device_id=(k * 2 + core, z), device_id_type=MESH)

    def block(owner, t):
        return grads[:, pl.ds(pl.multiple_of(owner * rows, rows), rows), pl.ds(pl.multiple_of(t * tile, tile), tile)]

    def core_stage(t):
        for k in range(n_chip):
            sib_out[t, k] = block(k * 2 + (1 - core), t).astype(b16)
        sib_copy(t).start()

    def chip_stage(t):
        sib_copy(t).wait_recv()
        for i in range(1, n_chip):
            k = other_chip(i)
            chip_out[t, k] = (block(k * 2 + core, t) + sib_in[t, k].astype(f32)).astype(b16)
            chip_copy(t, k).start()

    @pl.when(z < n_mp - 1)
    def _():
        for piece in range(2):
            tok_copy(z, piece, 0, z + 1).start()

    @pl.when(z > 0)
    def _():
        for piece in range(2):
            tok_copy(z, piece, 1, z - 1).start()

    for i in range(1, n_chip):
        k = other_chip(i)
        weight_copy(dp, w_send.at[k], k * 2 + core).start()
    weight_copy(dp, w_sib.at[chip], sibling).start()

    def clear(i, carry):
        part = pl.ds(pl.multiple_of(i * rows, rows), rows)
        grads[:, part, :] = jnp.zeros((2, rows, hidden_units), f32)
        return carry

    lax.fori_loop(0, n_dp, clear, 0)

    for i in range(1, n_chip):
        owner = other_chip(i) * 2 + core
        weight_copy(owner, w_sib.at[other_chip(i)], sibling).wait_recv()
        weight_copy(owner, w_sib.at[other_chip(i)], sibling).start()

    def pass_on(distance):
        for piece in range(2):
            @pl.when(z - distance >= 0)
            def _():
                tok_copy(z - distance, piece, 0, z).wait_recv()

                @pl.when(z < n_mp - 1)
                def _():
                    tok_copy(z - distance, piece, 0, z + 1).start()

            @pl.when(z + distance < n_mp)
            def _():
                tok_copy(z + distance, piece, 1, z).wait_recv()

                @pl.when(z > 0)
                def _():
                    tok_copy(z + distance, piece, 1, z - 1).start()

    pass_on(1)
    for k in range(n_chip):
        weight_copy(k * 2 + (1 - core), w_sib.at[k], sibling).wait_recv()

    furthest = jnp.where(z > n_mp - 1 - z, z, n_mp - 1 - z)
    at_end = (z == 0) | (z == n_mp - 1)

    def chunk(origin, last):
        flipped[0] = held[origin, 0].T
        flipped[1] = held[origin, 1].T

        def columns(step, carry):
            part = pl.ds(pl.multiple_of(step * tile, tile), tile)
            w_in = weights[0, :, part]
            preact = jnp.dot(held[origin, 0], w_in, preferred_element_type=f32)
            d_hidden = jnp.dot(held[origin, 1], weights[1, :, part], preferred_element_type=f32)
            hidden, slope = gelu_pair(preact)
            d_preact = (d_hidden * slope).astype(b16)
            grads[0, :, part] += jnp.dot(flipped[0], d_preact, preferred_element_type=f32)
            grads[1, :, part] += jnp.dot(flipped[1], hidden.astype(b16), preferred_element_type=f32)
            back = lax.dot_general(d_preact, w_in, (((1,), (1,)), ((), ())), preferred_element_type=f32)

            @pl.when(step == 0)
            def _():
                dn[...] = back

            @pl.when(step > 0)
            def _():
                dn[...] += back

            @pl.when(last)
            def _():
                core_stage(step)

                @pl.when(step > 0)
                def _():
                    chip_stage(step - 1)
            return carry

        lax.fori_loop(0, n_tile, columns, 0)

        @pl.when(origin == z)
        def _():
            own[...] = dn[...]

        @pl.when(origin != z)
        def _():
            ret_out[origin] = dn[...].astype(b16)

            @pl.when(at_end)
            def _():
                for step in range(n_ret):
                    ret_copy(origin, step, jnp.where(z == 0, 1, -1)).start()

    def at_distance(distance, carry):
        @pl.when(distance >= 2)
        def _():
            pass_on(distance)

        def side(which, inner):
            origin = z + distance * (2 * which - 1)

            @pl.when((origin >= 0) & (origin < n_mp) & (distance + which > 0))
            def _():
                chunk(origin, (distance == furthest) & ((which == 1) | (z + distance >= n_mp)))
            return inner

        lax.fori_loop(jnp.where(distance == 0, 1, 0), 2, side, 0)
        return carry

    lax.fori_loop(0, n_mp, at_distance, 0)

    chip_stage(n_tile - 1)

    def hand_on(far, carry):
        for step in range(n_ret):
            for turn in range(2):
                down = (turn + z // (n_mp // 2)) % 2
                way = 1 - 2 * down
                target = far + down * (n_mp - 1 - 2 * far)

                @pl.when(((target - z) * way > 0) & jnp.logical_not(at_end))
                def _():
                    part = pl.ds(step * ret_rows, ret_rows)
                    ret_arrival(target, step).wait_recv()
                    ret_out[target, part] = (
                        ret_out[target, part].astype(f32) + ret_in[target, part].astype(f32)
                    ).astype(b16)
                    ret_copy(target, step, way).start()
        return carry

    lax.fori_loop(1, n_mp, hand_on, 0)

    for t in range(n_tile):
        total = block(dp, t) + sib_in[t, chip].astype(f32)
        for i in range(1, n_chip):
            k = other_chip(i)
            chip_arrival(t, k).wait_recv()
            total += chip_in[t, k].astype(f32)
        gin_ref[:, t * tile:(t + 1) * tile] = total[0]
        gout_ref[t * tile:(t + 1) * tile, :] = total[1].T

    @pl.when(z < n_mp - 1)
    def _():
        for step in range(n_ret):
            ret_arrival(z, step).wait_recv()
        own[...] += ret_in[z].astype(f32)

    @pl.when(z > 0)
    def _():
        for step in range(n_ret):
            ret_arrival(n_mp, step).wait_recv()
        own[...] += ret_in[n_mp].astype(f32)

    values = tokens_ref[...].astype(f32)
    inverse = lax.rsqrt(jnp.mean(values * values, axis=-1, keepdims=True) + 1e-06)
    normed = values * inverse
    d_normed = own[...]
    d_rows = inverse * (d_normed - normed * jnp.mean(d_normed * normed, axis=-1, keepdims=True))
    ig_ref[...] = d_rows.astype(b16)

    for i in range(1, n_chip):
        k = other_chip(i)
        weight_copy(dp, w_send.at[k], k * 2 + core).wait_send()
        for t in range(n_tile):
            chip_copy(t, k).wait_send()
    for k in range(n_chip):
        weight_copy(k * 2 + core, w_sib.at[k], sibling).wait_send()
    for t in range(n_tile):
        sib_copy(t).wait_send()
    for origin in range(n_mp):
        for piece in range(2):
            @pl.when((z < n_mp - 1) & (origin <= z))
            def _():
                tok_copy(origin, piece, 0, z + 1).wait_send()

            @pl.when((z > 0) & (origin >= z))
            def _():
                tok_copy(origin, piece, 1, z - 1).wait_send()
    for i in range(1, n_mp):
        target = (z + i) % n_mp
        for step in range(n_ret):
            ret_copy(target, step, jnp.where(target > z, 1, -1)).wait_send()


def shards(n_dp, n_mp, tokens, cotangent, weight_in, weight_out, moment_in, second_in, moment_out, second_out):
    count, width = tokens.shape
    rows, units = weight_in.shape
    n_chip = n_dp // 2
    n_ret = 4
    tile = min(256, units)
    n_tile = units // tile
    b16, f32 = jnp.bfloat16, jnp.float32
    vmem = pl.BlockSpec(memory_space=pltpu.VMEM)
    dma = pltpu.SemaphoreType.DMA
    flops = 10 * count * n_mp * width * units
    input_grad, grad_in, grad_out = pl.pallas_call(
        functools.partial(kernel, n_dp, n_mp, tile),
        out_shape=(
            jax.ShapeDtypeStruct((count, width), b16),
            jax.ShapeDtypeStruct((rows, units), f32),
            jax.ShapeDtypeStruct((units, rows), f32),
        ),
        in_specs=[vmem] * 4,
        out_specs=(vmem,) * 3,
        scratch_shapes=[
            pltpu.VMEM((n_mp, 2, count, width), b16),
            pltpu.VMEM((2, width, units), b16),
            pltpu.VMEM((2, width, units), f32),
            pltpu.VMEM((2, width, count), b16),
            pltpu.VMEM((count, width), f32),
            pltpu.VMEM((count, width), f32),
            pltpu.VMEM((n_mp, count, width), b16),
            pltpu.VMEM((n_mp + 1, count, width), b16),
            pltpu.VMEM((n_tile, n_chip, 2, rows, tile), b16),
            pltpu.VMEM((n_tile, n_chip, 2, rows, tile), b16),
            pltpu.VMEM((n_tile, n_chip, 2, rows, tile), b16),
            pltpu.VMEM((n_tile, n_chip, 2, rows, tile), b16),
            dma((2, n_mp, 2)), dma((n_mp, 2)),
            dma((n_chip,)), dma((n_chip,)), dma((n_dp,)),
            dma((n_mp, n_ret)), dma((n_mp + 1, n_ret)),
            dma((n_tile,)), dma((n_tile,)),
            dma((n_tile, n_chip)), dma((n_tile, n_chip)),
        ],
        compiler_params=pltpu.CompilerParams(
            collective_id=0, has_side_effects=True, vmem_limit_bytes=56 * 1024 * 1024
        ),
        cost_estimate=pl.CostEstimate(flops=flops, bytes_accessed=8 * rows * units * 4, transcendentals=0),
    )(tokens, cotangent, weight_in, weight_out)
    grad_scale = 1.0 / jnp.sqrt(jnp.float32(count * n_dp * n_mp))
    new_in = adam_step(weight_in, moment_in, second_in, grad_in * grad_scale)
    new_out = adam_step(weight_out, moment_out, second_out, grad_out * grad_scale)
    return (input_grad, *new_in, *new_out)


def solution(mesh):
    return jax.shard_map(
        functools.partial(shards, mesh.shape["dp"], mesh.shape["mp"]),
        mesh=mesh,
        in_specs=(
            P(("dp", "mp"), None),
            P(("dp", "mp"), None),
            P("dp", "mp"),
            P("mp", "dp"),
            P("dp", "mp"),
            P("dp", "mp"),
            P("mp", "dp"),
            P("mp", "dp"),
        ),
        out_specs=(
            P(("dp", "mp"), None),
            P("dp", "mp"),
            P("dp", "mp"),
            P("dp", "mp"),
            P("mp", "dp"),
            P("mp", "dp"),
            P("mp", "dp"),
        ),
        check_vma=False,
    )
```

```python
import functools
import math

import jax
import jax.numpy as jnp
from jax import lax
from jax.experimental import pallas as pl
from jax.experimental.pallas import tpu as pltpu
from jax.sharding import PartitionSpec as P

MESH = pl.DeviceIdType.MESH
STEP = 1000

BETA_ONE = 0.9
BETA_TWO = 0.999
EPSILON = 1e-08
LEARN_RATE = 0.001
DECAY_RATE = 0.1
CUBIC = 0.044715
ROOT = math.sqrt(2.0 / math.pi)


def adam_step(weight, moment, second, gradient):
    moment_new = BETA_ONE * moment + (1.0 - BETA_ONE) * gradient
    second_new = BETA_TWO * second + (1.0 - BETA_TWO) * gradient * gradient
    first_fix = 1.0 - BETA_ONE ** float(STEP)
    second_fix = 1.0 - BETA_TWO ** float(STEP)
    update = moment_new / first_fix / (jnp.sqrt(second_new / second_fix) + EPSILON)
    weight_new = weight - LEARN_RATE * (update + DECAY_RATE * weight)
    return (weight_new, moment_new, second_new)


def gelu_pair(v):
    square = v * v
    t = jnp.tanh(ROOT * (v + CUBIC * (square * v)))
    half = 0.5 * (1.0 + t)
    slope = half + (0.5 * ROOT) * v * (1.0 - t * t) * (1.0 + (3.0 * CUBIC) * square)
    return v * half, slope


def kernel(
    n_dp, n_mp, tile,
    tokens_ref, cot_ref, win_ref, wout_ref,
    ig_ref, gin_ref, gout_ref,
    held, weights, grads, flipped, dn, own, ret_out, ret_in, sib_out, sib_in, chip_out, chip_in,
    tok_send, tok_recv, w_send, w_sib, w_recv, ret_send, ret_recv, sib_send, sib_recv, chip_send, chip_recv,
):
    n_chip = n_dp // 2
    dp, z = lax.axis_index("dp"), lax.axis_index("mp")
    chip, core = dp // 2, dp % 2
    sibling = chip * 2 + (1 - core)
    rows = win_ref.shape[0]
    hidden_units = win_ref.shape[1]
    f32, b16 = jnp.float32, jnp.bfloat16
    n_tile = hidden_units // tile
    n_ret = ret_send.shape[1]
    ret_rows = tokens_ref.shape[0] // n_ret

    def other_chip(i):
        return (chip + i) % n_chip

    barrier = pltpu.get_barrier_semaphore()
    pl.semaphore_signal(barrier, inc=1, device_id=(sibling, z), device_id_type=MESH)
    for i in range(1, n_chip):
        pl.semaphore_signal(barrier, inc=1, device_id=(other_chip(i) * 2 + core, z), device_id_type=MESH)
    for i in range(1, n_mp):
        pl.semaphore_signal(barrier, inc=1, device_id=(dp, (z + i) % n_mp), device_id_type=MESH)

    def tok_copy(origin, piece, side, target):
        return pltpu.make_async_remote_copy(
            src_ref=held.at[origin, piece], dst_ref=held.at[origin, piece],
            send_sem=tok_send.at[side, origin, piece], recv_sem=tok_recv.at[origin, piece],
            device_id=(dp, target), device_id_type=MESH)

    def weight_copy(owner, send_sem, target):
        block = weights.at[:, pl.ds(pl.multiple_of(owner * rows, rows), rows), :]
        return pltpu.make_async_remote_copy(
            src_ref=block, dst_ref=block, send_sem=send_sem, recv_sem=w_recv.at[owner],
            device_id=(target, z), device_id_type=MESH)

    def ret_copy(target, step, way):
        part = pl.ds(step * ret_rows, ret_rows)
        slot = jnp.where((z + way == target) & (way == 1), n_mp, target)
        return pltpu.make_async_remote_copy(
            src_ref=ret_out.at[target, part], dst_ref=ret_in.at[slot, part],
            send_sem=ret_send.at[target, step], recv_sem=ret_recv.at[slot, step],
            device_id=(dp, z + way), device_id_type=MESH)

    def ret_arrival(slot, step):
        part = pl.ds(step * ret_rows, ret_rows)
        return pltpu.make_async_remote_copy(
            src_ref=ret_in.at[slot, part], dst_ref=ret_in.at[slot, part],
            send_sem=ret_send.at[0, step], recv_sem=ret_recv.at[slot, step],
            device_id=(dp, z), device_id_type=MESH)

    def sib_copy(t):
        return pltpu.make_async_remote_copy(
            src_ref=sib_out.at[t], dst_ref=sib_in.at[t],
            send_sem=sib_send.at[t], recv_sem=sib_recv.at[t],
            device_id=(sibling, z), device_id_type=MESH)

    def chip_copy(t, k):
        return pltpu.make_async_remote_copy(
            src_ref=chip_out.at[t, k], dst_ref=chip_in.at[t, chip],
            send_sem=chip_send.at[t, k], recv_sem=chip_recv.at[t, chip],
            device_id=(k * 2 + core, z), device_id_type=MESH)

    def chip_arrival(t, k):
        return pltpu.make_async_remote_copy(
            src_ref=chip_in.at[t, k], dst_ref=chip_in.at[t, k],
            send_sem=chip_send.at[t, k], recv_sem=chip_recv.at[t, k],
            device_id=(k * 2 + core, z), device_id_type=MESH)

    def block(owner, t):
        return grads[:, pl.ds(pl.multiple_of(owner * rows, rows), rows), pl.ds(pl.multiple_of(t * tile, tile), tile)]

    def core_stage(t):
        for k in range(n_chip):
            sib_out[t, k] = block(k * 2 + (1 - core), t).astype(b16)
        sib_copy(t).start()

    def chip_stage(t):
        sib_copy(t).wait_recv()
        for i in range(1, n_chip):
            k = other_chip(i)
            chip_out[t, k] = (block(k * 2 + core, t) + sib_in[t, k].astype(f32)).astype(b16)
            chip_copy(t, k).start()

    def send_own(piece):
        @pl.when(z < n_mp - 1)
        def _():
            tok_copy(z, piece, 0, z + 1).start()

        @pl.when(z > 0)
        def _():
            tok_copy(z, piece, 1, z - 1).start()

    held[z, 1] = cot_ref[...]
    own_rows = pl.ds(pl.multiple_of(dp * rows, rows), rows)
    weights[0, own_rows, :] = win_ref[...].astype(b16)
    weights[1, own_rows, :] = wout_ref[...].T.astype(b16)
    pl.semaphore_wait(barrier, n_chip + n_mp - 1)
    send_own(1)
    for i in range(1, n_chip):
        k = other_chip(i)
        weight_copy(dp, w_send.at[k], k * 2 + core).start()
    weight_copy(dp, w_sib.at[chip], sibling).start()
    values = tokens_ref[...].astype(f32)
    inverse = lax.rsqrt(jnp.mean(values * values, axis=-1, keepdims=True) + 1e-06)
    held[z, 0] = (values * inverse).astype(b16)
    send_own(0)

    def clear(i, carry):
        part = pl.ds(pl.multiple_of(i * rows, rows), rows)
        grads[:, part, :] = jnp.zeros((2, rows, hidden_units), f32)
        return carry

    lax.fori_loop(0, n_dp, clear, 0)

    for i in range(1, n_chip):
        owner = other_chip(i) * 2 + core
        weight_copy(owner, w_sib.at[other_chip(i)], sibling).wait_recv()
        weight_copy(owner, w_sib.at[other_chip(i)], sibling).start()

    def pass_on(distance):
        for piece in (1, 0):
            @pl.when(z - distance >= 0)
            def _():
                tok_copy(z - distance, piece, 0, z).wait_recv()

                @pl.when(z < n_mp - 1)
                def _():
                    tok_copy(z - distance, piece, 0, z + 1).start()

            @pl.when(z + distance < n_mp)
            def _():
                tok_copy(z + distance, piece, 1, z).wait_recv()

                @pl.when(z > 0)
                def _():
                    tok_copy(z + distance, piece, 1, z - 1).start()

    at_end = (z == 0) | (z == n_mp - 1)

    @pl.when(jnp.logical_not(at_end))
    def _():
        pass_on(1)

    for k in range(n_chip):
        weight_copy(k * 2 + (1 - core), w_sib.at[k], sibling).wait_recv()

    furthest = jnp.where(z > n_mp - 1 - z, z, n_mp - 1 - z)

    def chunk(origin, last):
        flipped[0] = held[origin, 0].T
        flipped[1] = held[origin, 1].T

        def columns(step, carry):
            part = pl.ds(pl.multiple_of(step * tile, tile), tile)
            w_in = weights[0, :, part]
            preact = jnp.dot(held[origin, 0], w_in, preferred_element_type=f32)
            d_hidden = jnp.dot(held[origin, 1], weights[1, :, part], preferred_element_type=f32)
            hidden, slope = gelu_pair(preact)
            d_preact = (d_hidden * slope).astype(b16)
            grads[0, :, part] += jnp.dot(flipped[0], d_preact, preferred_element_type=f32)
            grads[1, :, part] += jnp.dot(flipped[1], hidden.astype(b16), preferred_element_type=f32)
            back = lax.dot_general(d_preact, w_in, (((1,), (1,)), ((), ())), preferred_element_type=f32)

            @pl.when(step == 0)
            def _():
                dn[...] = back

            @pl.when(step > 0)
            def _():
                dn[...] += back

            @pl.when(last)
            def _():
                core_stage(step)

                @pl.when(step > 0)
                def _():
                    chip_stage(step - 1)
            return carry

        lax.fori_loop(0, n_tile, columns, 0)

        @pl.when(origin == z)
        def _():
            own[...] = dn[...]

        @pl.when(origin != z)
        def _():
            ret_out[origin] = dn[...].astype(b16)

            @pl.when(at_end)
            def _():
                for step in range(n_ret):
                    ret_copy(origin, step, jnp.where(z == 0, 1, -1)).start()

    def at_distance(distance, carry):
        ahead = distance + jnp.where(at_end, 0, 1)

        @pl.when((distance >= 1) & (ahead < n_mp))
        def _():
            pass_on(ahead)

        def side(which, inner):
            origin = z + distance * (2 * which - 1)

            @pl.when((origin >= 0) & (origin < n_mp) & (distance + which > 0))
            def _():
                chunk(origin, (distance == furthest) & ((which == 1) | (z + distance >= n_mp)))
            return inner

        lax.fori_loop(jnp.where(distance == 0, 1, 0), 2, side, 0)
        return carry

    lax.fori_loop(0, n_mp, at_distance, 0)

    chip_stage(n_tile - 1)

    def hand_on(far, carry):
        for step in range(n_ret):
            for turn in range(2):
                down = (turn + z // (n_mp // 2)) % 2
                way = 1 - 2 * down
                target = far + down * (n_mp - 1 - 2 * far)

                @pl.when(((target - z) * way > 0) & jnp.logical_not(at_end))
                def _():
                    part = pl.ds(step * ret_rows, ret_rows)
                    ret_arrival(target, step).wait_recv()
                    ret_out[target, part] = (
                        ret_out[target, part].astype(f32) + ret_in[target, part].astype(f32)
                    ).astype(b16)
                    ret_copy(target, step, way).start()
        return carry

    lax.fori_loop(1, n_mp, hand_on, 0)

    for t in range(n_tile):
        total = block(dp, t) + sib_in[t, chip].astype(f32)
        for i in range(1, n_chip):
            k = other_chip(i)
            chip_arrival(t, k).wait_recv()
            total += chip_in[t, k].astype(f32)
        gin_ref[:, t * tile:(t + 1) * tile] = total[0]
        gout_ref[t * tile:(t + 1) * tile, :] = total[1].T

    @pl.when(z < n_mp - 1)
    def _():
        for step in range(n_ret):
            ret_arrival(z, step).wait_recv()
        own[...] += ret_in[z].astype(f32)

    @pl.when(z > 0)
    def _():
        for step in range(n_ret):
            ret_arrival(n_mp, step).wait_recv()
        own[...] += ret_in[n_mp].astype(f32)

    values = tokens_ref[...].astype(f32)
    inverse = lax.rsqrt(jnp.mean(values * values, axis=-1, keepdims=True) + 1e-06)
    normed = values * inverse
    d_normed = own[...]
    d_rows = inverse * (d_normed - normed * jnp.mean(d_normed * normed, axis=-1, keepdims=True))
    ig_ref[...] = d_rows.astype(b16)

    for i in range(1, n_chip):
        k = other_chip(i)
        weight_copy(dp, w_send.at[k], k * 2 + core).wait_send()
        for t in range(n_tile):
            chip_copy(t, k).wait_send()
    for k in range(n_chip):
        weight_copy(k * 2 + core, w_sib.at[k], sibling).wait_send()
    for t in range(n_tile):
        sib_copy(t).wait_send()
    for origin in range(n_mp):
        for piece in range(2):
            @pl.when((z < n_mp - 1) & (origin <= z))
            def _():
                tok_copy(origin, piece, 0, z + 1).wait_send()

            @pl.when((z > 0) & (origin >= z))
            def _():
                tok_copy(origin, piece, 1, z - 1).wait_send()
    for i in range(1, n_mp):
        target = (z + i) % n_mp
        for step in range(n_ret):
            ret_copy(target, step, jnp.where(target > z, 1, -1)).wait_send()


def shards(n_dp, n_mp, tokens, cotangent, weight_in, weight_out, moment_in, second_in, moment_out, second_out):
    count, width = tokens.shape
    rows, units = weight_in.shape
    n_chip = n_dp // 2
    n_ret = 8
    tile = min(256, units)
    n_tile = units // tile
    b16, f32 = jnp.bfloat16, jnp.float32
    vmem = pl.BlockSpec(memory_space=pltpu.VMEM)
    dma = pltpu.SemaphoreType.DMA
    flops = 10 * count * n_mp * width * units
    input_grad, grad_in, grad_out = pl.pallas_call(
        functools.partial(kernel, n_dp, n_mp, tile),
        out_shape=(
            jax.ShapeDtypeStruct((count, width), b16),
            jax.ShapeDtypeStruct((rows, units), f32),
            jax.ShapeDtypeStruct((units, rows), f32),
        ),
        in_specs=[vmem] * 4,
        out_specs=(vmem,) * 3,
        scratch_shapes=[
            pltpu.VMEM((n_mp, 2, count, width), b16),
            pltpu.VMEM((2, width, units), b16),
            pltpu.VMEM((2, width, units), f32),
            pltpu.VMEM((2, width, count), b16),
            pltpu.VMEM((count, width), f32),
            pltpu.VMEM((count, width), f32),
            pltpu.VMEM((n_mp, count, width), b16),
            pltpu.VMEM((n_mp + 1, count, width), b16),
            pltpu.VMEM((n_tile, n_chip, 2, rows, tile), b16),
            pltpu.VMEM((n_tile, n_chip, 2, rows, tile), b16),
            pltpu.VMEM((n_tile, n_chip, 2, rows, tile), b16),
            pltpu.VMEM((n_tile, n_chip, 2, rows, tile), b16),
            dma((2, n_mp, 2)), dma((n_mp, 2)),
            dma((n_chip,)), dma((n_chip,)), dma((n_dp,)),
            dma((n_mp, n_ret)), dma((n_mp + 1, n_ret)),
            dma((n_tile,)), dma((n_tile,)),
            dma((n_tile, n_chip)), dma((n_tile, n_chip)),
        ],
        compiler_params=pltpu.CompilerParams(
            collective_id=0, has_side_effects=True, vmem_limit_bytes=56 * 1024 * 1024
        ),
        cost_estimate=pl.CostEstimate(flops=flops, bytes_accessed=8 * rows * units * 4, transcendentals=0),
    )(tokens, cotangent, weight_in, weight_out)
    grad_scale = 1.0 / jnp.sqrt(jnp.float32(count * n_dp * n_mp))
    new_in = adam_step(weight_in, moment_in, second_in, grad_in * grad_scale)
    new_out = adam_step(weight_out, moment_out, second_out, grad_out * grad_scale)
    return (input_grad, *new_in, *new_out)


def solution(mesh):
    return jax.shard_map(
        functools.partial(shards, mesh.shape["dp"], mesh.shape["mp"]),
        mesh=mesh,
        in_specs=(
            P(("dp", "mp"), None),
            P(("dp", "mp"), None),
            P("dp", "mp"),
            P("mp", "dp"),
            P("dp", "mp"),
            P("dp", "mp"),
            P("mp", "dp"),
            P("mp", "dp"),
        ),
        out_specs=(
            P(("dp", "mp"), None),
            P("dp", "mp"),
            P("dp", "mp"),
            P("dp", "mp"),
            P("mp", "dp"),
            P("mp", "dp"),
            P("mp", "dp"),
        ),
        check_vma=False,
    )
```

```python
import functools
import math

import jax
import jax.numpy as jnp
from jax import lax
from jax.experimental import pallas as pl
from jax.experimental.pallas import tpu as pltpu
from jax.sharding import PartitionSpec as P

MESH = pl.DeviceIdType.MESH
STEP = 1000

BETA_ONE = 0.9
BETA_TWO = 0.999
EPSILON = 1e-08
LEARN_RATE = 0.001
DECAY_RATE = 0.1
CUBIC = 0.044715
ROOT = math.sqrt(2.0 / math.pi)


def adam_step(weight, moment, second, gradient):
    moment_new = BETA_ONE * moment + (1.0 - BETA_ONE) * gradient
    second_new = BETA_TWO * second + (1.0 - BETA_TWO) * gradient * gradient
    first_fix = 1.0 - BETA_ONE ** float(STEP)
    second_fix = 1.0 - BETA_TWO ** float(STEP)
    update = moment_new / first_fix / (jnp.sqrt(second_new / second_fix) + EPSILON)
    weight_new = weight - LEARN_RATE * (update + DECAY_RATE * weight)
    return (weight_new, moment_new, second_new)


def update(scale, ig_ref, *refs):
    gin, win, min_, sin, gout, wout, mout, sout, ig_new, *new = refs
    ig_new[...] = ig_ref[...]
    for place, group in ((0, (win, min_, sin, gin)), (3, (wout, mout, sout, gout))):
        weight, moment, second, gradient = (ref[...] for ref in group)
        results = adam_step(weight, moment, second, gradient * scale)
        for offset, result in enumerate(results):
            new[place + offset][...] = result


def gelu_pair(v):
    square = v * v
    t = jnp.tanh(ROOT * (v + CUBIC * (square * v)))
    half = 0.5 * (1.0 + t)
    slope = half + (0.5 * ROOT) * v * (1.0 - t * t) * (1.0 + (3.0 * CUBIC) * square)
    return v * half, slope


def kernel(
    n_dp, n_mp, tile,
    tokens_ref, cot_ref, win_ref, wout_ref,
    ig_ref, gin_ref, gout_ref,
    held, weights, grads, flipped, win_t, d_pre, own, ret_out, ret_in, sib_out, sib_in, chip_out, chip_in,
    tok_send, tok_recv, w_send, w_sib, w_recv, ret_send, ret_recv, sib_send, sib_recv, chip_send, chip_recv,
):
    n_chip = n_dp // 2
    dp, z = lax.axis_index("dp"), lax.axis_index("mp")
    chip, core = dp // 2, dp % 2
    sibling = chip * 2 + (1 - core)
    rows = win_ref.shape[0]
    hidden_units = win_ref.shape[1]
    f32, b16 = jnp.float32, jnp.bfloat16
    n_tile = hidden_units // tile
    width = tokens_ref.shape[1]
    wide = min(256, width)
    n_wide = width // wide
    n_ret = ret_send.shape[1]
    ret_rows = tokens_ref.shape[0] // n_ret

    def other_chip(i):
        return (chip + i) % n_chip

    barrier = pltpu.get_barrier_semaphore()
    pl.semaphore_signal(barrier, inc=1, device_id=(sibling, z), device_id_type=MESH)
    for i in range(1, n_chip):
        pl.semaphore_signal(barrier, inc=1, device_id=(other_chip(i) * 2 + core, z), device_id_type=MESH)
    for i in range(1, n_mp):
        pl.semaphore_signal(barrier, inc=1, device_id=(dp, (z + i) % n_mp), device_id_type=MESH)

    def tok_copy(origin, piece, side, target):
        return pltpu.make_async_remote_copy(
            src_ref=held.at[origin, piece], dst_ref=held.at[origin, piece],
            send_sem=tok_send.at[side, origin, piece], recv_sem=tok_recv.at[origin, piece],
            device_id=(dp, target), device_id_type=MESH)

    def weight_copy(owner, send_sem, target):
        block = weights.at[:, pl.ds(pl.multiple_of(owner * rows, rows), rows), :]
        return pltpu.make_async_remote_copy(
            src_ref=block, dst_ref=block, send_sem=send_sem, recv_sem=w_recv.at[owner],
            device_id=(target, z), device_id_type=MESH)

    def ret_copy(target, step, way):
        part = pl.ds(step * ret_rows, ret_rows)
        slot = jnp.where((z + way == target) & (way == 1), n_mp, target)
        return pltpu.make_async_remote_copy(
            src_ref=ret_out.at[target, part], dst_ref=ret_in.at[slot, part],
            send_sem=ret_send.at[target, step], recv_sem=ret_recv.at[slot, step],
            device_id=(dp, z + way), device_id_type=MESH)

    def ret_arrival(slot, step):
        part = pl.ds(step * ret_rows, ret_rows)
        return pltpu.make_async_remote_copy(
            src_ref=ret_in.at[slot, part], dst_ref=ret_in.at[slot, part],
            send_sem=ret_send.at[0, step], recv_sem=ret_recv.at[slot, step],
            device_id=(dp, z), device_id_type=MESH)

    def sib_copy(t):
        return pltpu.make_async_remote_copy(
            src_ref=sib_out.at[t], dst_ref=sib_in.at[t],
            send_sem=sib_send.at[t], recv_sem=sib_recv.at[t],
            device_id=(sibling, z), device_id_type=MESH)

    def chip_copy(t, k):
        return pltpu.make_async_remote_copy(
            src_ref=chip_out.at[t, k], dst_ref=chip_in.at[t, chip],
            send_sem=chip_send.at[t, k], recv_sem=chip_recv.at[t, chip],
            device_id=(k * 2 + core, z), device_id_type=MESH)

    def chip_arrival(t, k):
        return pltpu.make_async_remote_copy(
            src_ref=chip_in.at[t, k], dst_ref=chip_in.at[t, k],
            send_sem=chip_send.at[t, k], recv_sem=chip_recv.at[t, k],
            device_id=(k * 2 + core, z), device_id_type=MESH)

    def block(owner, t):
        return grads[:, pl.ds(pl.multiple_of(owner * rows, rows), rows), pl.ds(pl.multiple_of(t * tile, tile), tile)]

    def core_stage(t):
        for k in range(n_chip):
            sib_out[t, k] = block(k * 2 + (1 - core), t).astype(b16)
        sib_copy(t).start()

    def chip_stage(t):
        sib_copy(t).wait_recv()
        for i in range(1, n_chip):
            k = other_chip(i)
            chip_out[t, k] = (block(k * 2 + core, t) + sib_in[t, k].astype(f32)).astype(b16)
            chip_copy(t, k).start()

    def send_own(piece):
        @pl.when(z < n_mp - 1)
        def _():
            tok_copy(z, piece, 0, z + 1).start()

        @pl.when(z > 0)
        def _():
            tok_copy(z, piece, 1, z - 1).start()

    held[z, 1] = cot_ref[...]
    own_rows = pl.ds(pl.multiple_of(dp * rows, rows), rows)
    weights[0, own_rows, :] = win_ref[...].astype(b16)
    weights[1, own_rows, :] = wout_ref[...].T.astype(b16)
    pl.semaphore_wait(barrier, n_chip + n_mp - 1)
    send_own(1)
    for i in range(1, n_chip):
        k = other_chip(i)
        weight_copy(dp, w_send.at[k], k * 2 + core).start()
    weight_copy(dp, w_sib.at[chip], sibling).start()
    values = tokens_ref[...].astype(f32)
    inverse = lax.rsqrt(jnp.mean(values * values, axis=-1, keepdims=True) + 1e-06)
    held[z, 0] = (values * inverse).astype(b16)
    send_own(0)

    def clear(i, carry):
        part = pl.ds(pl.multiple_of(i * rows, rows), rows)
        grads[:, part, :] = jnp.zeros((2, rows, hidden_units), f32)
        return carry

    lax.fori_loop(0, n_dp, clear, 0)

    for i in range(1, n_chip):
        owner = other_chip(i) * 2 + core
        weight_copy(owner, w_sib.at[other_chip(i)], sibling).wait_recv()
        weight_copy(owner, w_sib.at[other_chip(i)], sibling).start()

    def pass_on(distance):
        for piece in (1, 0):
            @pl.when(z - distance >= 0)
            def _():
                tok_copy(z - distance, piece, 0, z).wait_recv()

                @pl.when(z < n_mp - 1)
                def _():
                    tok_copy(z - distance, piece, 0, z + 1).start()

            @pl.when(z + distance < n_mp)
            def _():
                tok_copy(z + distance, piece, 1, z).wait_recv()

                @pl.when(z > 0)
                def _():
                    tok_copy(z + distance, piece, 1, z - 1).start()

    at_end = (z == 0) | (z == n_mp - 1)

    pass_on(1)
    for k in range(n_chip):
        weight_copy(k * 2 + (1 - core), w_sib.at[k], sibling).wait_recv()

    def turn(step, carry):
        part = pl.ds(pl.multiple_of(step * wide, wide), wide)
        win_t[:, part] = weights[0, part, :].T
        return carry

    lax.fori_loop(0, n_wide, turn, 0)

    furthest = jnp.where(z > n_mp - 1 - z, z, n_mp - 1 - z)

    def chunk(origin, last):
        flipped[0] = held[origin, 0].T
        flipped[1] = held[origin, 1].T

        def columns(step, carry):
            part = pl.ds(pl.multiple_of(step * tile, tile), tile)
            preact = jnp.dot(held[origin, 0], weights[0, :, part], preferred_element_type=f32)
            d_hidden = jnp.dot(held[origin, 1], weights[1, :, part], preferred_element_type=f32)
            hidden, slope = gelu_pair(preact)
            d_preact = (d_hidden * slope).astype(b16)
            grads[0, :, part] += jnp.dot(flipped[0], d_preact, preferred_element_type=f32)
            grads[1, :, part] += jnp.dot(flipped[1], hidden.astype(b16), preferred_element_type=f32)
            d_pre[:, part] = d_preact

            @pl.when(last)
            def _():
                core_stage(step)

                @pl.when(step > 0)
                def _():
                    chip_stage(step - 1)
            return carry

        lax.fori_loop(0, n_tile, columns, 0)

        def back(step, carry):
            part = pl.ds(pl.multiple_of(step * wide, wide), wide)
            sums = jnp.dot(d_pre[...], win_t[:, part], preferred_element_type=f32)

            @pl.when(origin == z)
            def _():
                own[:, part] = sums

            @pl.when(origin != z)
            def _():
                ret_out[origin, :, part] = sums.astype(b16)
            return carry

        lax.fori_loop(0, n_wide, back, 0)

        @pl.when(origin != z)
        def _():
            @pl.when(at_end)
            def _():
                for step in range(n_ret):
                    ret_copy(origin, step, jnp.where(z == 0, 1, -1)).start()

    def at_distance(distance, carry):
        @pl.when(distance >= 2)
        def _():
            pass_on(distance)

        def side(which, inner):
            origin = z + distance * (2 * which - 1)

            @pl.when((origin >= 0) & (origin < n_mp) & (distance + which > 0))
            def _():
                chunk(origin, (distance == furthest) & ((which == 1) | (z + distance >= n_mp)))
            return inner

        lax.fori_loop(jnp.where(distance == 0, 1, 0), 2, side, 0)
        return carry

    lax.fori_loop(0, n_mp, at_distance, 0)

    chip_stage(n_tile - 1)

    def hand_on(far, carry):
        for step in range(n_ret):
            for turn in range(2):
                down = (turn + z // (n_mp // 2)) % 2
                way = 1 - 2 * down
                target = far + down * (n_mp - 1 - 2 * far)

                @pl.when(((target - z) * way > 0) & jnp.logical_not(at_end))
                def _():
                    part = pl.ds(step * ret_rows, ret_rows)
                    ret_arrival(target, step).wait_recv()
                    ret_out[target, part] = (
                        ret_out[target, part].astype(f32) + ret_in[target, part].astype(f32)
                    ).astype(b16)
                    ret_copy(target, step, way).start()
        return carry

    lax.fori_loop(1, n_mp, hand_on, 0)

    for t in range(n_tile):
        total = block(dp, t) + sib_in[t, chip].astype(f32)
        for i in range(1, n_chip):
            k = other_chip(i)
            chip_arrival(t, k).wait_recv()
            total += chip_in[t, k].astype(f32)
        gin_ref[:, t * tile:(t + 1) * tile] = total[0]
        gout_ref[t * tile:(t + 1) * tile, :] = total[1].T

    @pl.when(z < n_mp - 1)
    def _():
        for step in range(n_ret):
            ret_arrival(z, step).wait_recv()
        own[...] += ret_in[z].astype(f32)

    @pl.when(z > 0)
    def _():
        for step in range(n_ret):
            ret_arrival(n_mp, step).wait_recv()
        own[...] += ret_in[n_mp].astype(f32)

    values = tokens_ref[...].astype(f32)
    inverse = lax.rsqrt(jnp.mean(values * values, axis=-1, keepdims=True) + 1e-06)
    normed = values * inverse
    d_normed = own[...]
    d_rows = inverse * (d_normed - normed * jnp.mean(d_normed * normed, axis=-1, keepdims=True))
    ig_ref[...] = d_rows.astype(b16)

    for i in range(1, n_chip):
        k = other_chip(i)
        weight_copy(dp, w_send.at[k], k * 2 + core).wait_send()
        for t in range(n_tile):
            chip_copy(t, k).wait_send()
    for k in range(n_chip):
        weight_copy(k * 2 + core, w_sib.at[k], sibling).wait_send()
    for t in range(n_tile):
        sib_copy(t).wait_send()
    for origin in range(n_mp):
        for piece in range(2):
            @pl.when((z < n_mp - 1) & (origin <= z))
            def _():
                tok_copy(origin, piece, 0, z + 1).wait_send()

            @pl.when((z > 0) & (origin >= z))
            def _():
                tok_copy(origin, piece, 1, z - 1).wait_send()
    for i in range(1, n_mp):
        target = (z + i) % n_mp
        for step in range(n_ret):
            ret_copy(target, step, jnp.where(target > z, 1, -1)).wait_send()


def shards(n_dp, n_mp, tokens, cotangent, weight_in, weight_out, moment_in, second_in, moment_out, second_out):
    count, width = tokens.shape
    rows, units = weight_in.shape
    n_chip = n_dp // 2
    n_ret = 4
    tile = min(256, units)
    n_tile = units // tile
    b16, f32 = jnp.bfloat16, jnp.float32
    vmem = pl.BlockSpec(memory_space=pltpu.VMEM)
    dma = pltpu.SemaphoreType.DMA
    flops = 10 * count * n_mp * width * units
    input_grad, grad_in, grad_out = pl.pallas_call(
        functools.partial(kernel, n_dp, n_mp, tile),
        out_shape=(
            jax.ShapeDtypeStruct((count, width), b16),
            jax.ShapeDtypeStruct((rows, units), f32),
            jax.ShapeDtypeStruct((units, rows), f32),
        ),
        in_specs=[vmem] * 4,
        out_specs=(vmem,) * 3,
        scratch_shapes=[
            pltpu.VMEM((n_mp, 2, count, width), b16),
            pltpu.VMEM((2, width, units), b16),
            pltpu.VMEM((2, width, units), f32),
            pltpu.VMEM((2, width, count), b16),
            pltpu.VMEM((units, width), b16),
            pltpu.VMEM((count, units), b16),
            pltpu.VMEM((count, width), f32),
            pltpu.VMEM((n_mp, count, width), b16),
            pltpu.VMEM((n_mp + 1, count, width), b16),
            pltpu.VMEM((n_tile, n_chip, 2, rows, tile), b16),
            pltpu.VMEM((n_tile, n_chip, 2, rows, tile), b16),
            pltpu.VMEM((n_tile, n_chip, 2, rows, tile), b16),
            pltpu.VMEM((n_tile, n_chip, 2, rows, tile), b16),
            dma((2, n_mp, 2)), dma((n_mp, 2)),
            dma((n_chip,)), dma((n_chip,)), dma((n_dp,)),
            dma((n_mp, n_ret)), dma((n_mp + 1, n_ret)),
            dma((n_tile,)), dma((n_tile,)),
            dma((n_tile, n_chip)), dma((n_tile, n_chip)),
        ],
        compiler_params=pltpu.CompilerParams(
            collective_id=0, has_side_effects=True, vmem_limit_bytes=56 * 1024 * 1024
        ),
        cost_estimate=pl.CostEstimate(flops=flops, bytes_accessed=8 * rows * units * 4, transcendentals=0),
    )(tokens, cotangent, weight_in, weight_out)
    n_step = 4
    across = pl.BlockSpec((rows, units // n_step), lambda i: (0, i))
    down = pl.BlockSpec((units // n_step, rows), lambda i: (i, 0))
    token_rows = pl.BlockSpec((count // n_step, width), lambda i: (i, 0))
    return pl.pallas_call(
        functools.partial(update, 1.0 / math.sqrt(count * n_dp * n_mp)),
        grid=(n_step,),
        out_shape=(jax.ShapeDtypeStruct((count, width), b16),)
        + (jax.ShapeDtypeStruct((rows, units), f32),) * 3
        + (jax.ShapeDtypeStruct((units, rows), f32),) * 3,
        in_specs=[token_rows] + [across] * 4 + [down] * 4,
        out_specs=(token_rows,) + (across,) * 3 + (down,) * 3,
        cost_estimate=pl.CostEstimate(flops=40 * rows * units, bytes_accessed=56 * rows * units, transcendentals=0),
    )(input_grad, grad_in, weight_in, moment_in, second_in, grad_out, weight_out, moment_out, second_out)


def solution(mesh):
    return jax.shard_map(
        functools.partial(shards, mesh.shape["dp"], mesh.shape["mp"]),
        mesh=mesh,
        in_specs=(
            P(("dp", "mp"), None),
            P(("dp", "mp"), None),
            P("dp", "mp"),
            P("mp", "dp"),
            P("dp", "mp"),
            P("dp", "mp"),
            P("mp", "dp"),
            P("mp", "dp"),
        ),
        out_specs=(
            P(("dp", "mp"), None),
            P("dp", "mp"),
            P("dp", "mp"),
            P("dp", "mp"),
            P("mp", "dp"),
            P("mp", "dp"),
            P("mp", "dp"),
        ),
        check_vma=False,
    )
```

```python
import functools
import math

import jax
import jax.numpy as jnp
from jax import lax
from jax.experimental import pallas as pl
from jax.experimental.pallas import tpu as pltpu
from jax.sharding import PartitionSpec as P

MESH = pl.DeviceIdType.MESH
STEP = 1000

BETA_ONE = 0.9
BETA_TWO = 0.999
EPSILON = 1e-08
LEARN_RATE = 0.001
DECAY_RATE = 0.1
CUBIC = 0.044715
ROOT = math.sqrt(2.0 / math.pi)


def adam_step(weight, moment, second, gradient):
    moment_new = BETA_ONE * moment + (1.0 - BETA_ONE) * gradient
    second_new = BETA_TWO * second + (1.0 - BETA_TWO) * gradient * gradient
    first_fix = 1.0 - BETA_ONE ** float(STEP)
    second_fix = 1.0 - BETA_TWO ** float(STEP)
    update = moment_new / first_fix / (jnp.sqrt(second_new / second_fix) + EPSILON)
    weight_new = weight - LEARN_RATE * (update + DECAY_RATE * weight)
    return (weight_new, moment_new, second_new)


def gelu_pair(v):
    square = v * v
    t = jnp.tanh(ROOT * (v + CUBIC * (square * v)))
    half = 0.5 * (1.0 + t)
    slope = half + (0.5 * ROOT) * v * (1.0 - t * t) * (1.0 + (3.0 * CUBIC) * square)
    return v * half, slope


def kernel(
    n_dp, n_mp, tile,
    tokens_ref, cot_ref, win_ref, wout_ref,
    ig_ref, gin_ref, gout_ref,
    held, weights, grads, flipped, dn, own, ret_out, ret_in, sib_out, sib_in, chip_out, chip_in,
    tok_send, tok_recv, w_send, w_relay, w_sib, w_recv, ret_send, ret_recv, sib_send, sib_recv, chip_send, chip_recv,
):
    n_chip = n_dp // 2
    dp, z = lax.axis_index("dp"), lax.axis_index("mp")
    chip, core = dp // 2, dp % 2
    sibling = chip * 2 + (1 - core)
    rows = win_ref.shape[0]
    hidden_units = win_ref.shape[1]
    f32, b16 = jnp.float32, jnp.bfloat16
    n_tile = hidden_units // tile
    n_ret = ret_send.shape[1]
    ret_rows = tokens_ref.shape[0] // n_ret

    def other_chip(i):
        return (chip + i) % n_chip

    barrier = pltpu.get_barrier_semaphore()
    pl.semaphore_signal(barrier, inc=1, device_id=(sibling, z), device_id_type=MESH)
    for i in range(1, n_chip):
        pl.semaphore_signal(barrier, inc=1, device_id=(other_chip(i) * 2 + core, z), device_id_type=MESH)
    for i in range(1, n_mp):
        pl.semaphore_signal(barrier, inc=1, device_id=(dp, (z + i) % n_mp), device_id_type=MESH)

    def tok_copy(origin, piece, side, target):
        return pltpu.make_async_remote_copy(
            src_ref=held.at[origin, piece], dst_ref=held.at[origin, piece],
            send_sem=tok_send.at[side, origin, piece], recv_sem=tok_recv.at[origin, piece],
            device_id=(dp, target), device_id_type=MESH)

    def weight_copy(owner, piece, send_sem, target):
        block = weights.at[piece, pl.ds(pl.multiple_of(owner * rows, rows), rows), :]
        return pltpu.make_async_remote_copy(
            src_ref=block, dst_ref=block, send_sem=send_sem, recv_sem=w_recv.at[owner, piece],
            device_id=(target, z), device_id_type=MESH)

    square = n_chip == 4
    near_x, near_y, diagonal = chip + 1 - 2 * (chip % 2), (chip + 2) % 4, 3 - chip
    if square:
        direct = [near_x, near_y]
        arrivals = [
            (near_x, 0, near_y), (near_y, 1, near_x), (near_x, 1, None),
            (near_y, 0, None), (diagonal, 0, None), (diagonal, 1, None),
        ]
    else:
        direct = [other_chip(i) for i in range(1, n_chip)]
        arrivals = [(k, piece, None) for k in direct for piece in range(2)]

    def ret_copy(target, step, way):
        part = pl.ds(step * ret_rows, ret_rows)
        slot = jnp.where((z + way == target) & (way == 1), n_mp, target)
        return pltpu.make_async_remote_copy(
            src_ref=ret_out.at[target, part], dst_ref=ret_in.at[slot, part],
            send_sem=ret_send.at[target, step], recv_sem=ret_recv.at[slot, step],
            device_id=(dp, z + way), device_id_type=MESH)

    def ret_arrival(slot, step):
        part = pl.ds(step * ret_rows, ret_rows)
        return pltpu.make_async_remote_copy(
            src_ref=ret_in.at[slot, part], dst_ref=ret_in.at[slot, part],
            send_sem=ret_send.at[0, step], recv_sem=ret_recv.at[slot, step],
            device_id=(dp, z), device_id_type=MESH)

    def sib_copy(t):
        return pltpu.make_async_remote_copy(
            src_ref=sib_out.at[t], dst_ref=sib_in.at[t],
            send_sem=sib_send.at[t], recv_sem=sib_recv.at[t],
            device_id=(sibling, z), device_id_type=MESH)

    def chip_copy(t, k, piece):
        target, slot = k, chip
        if k is diagonal and square:
            target = near_y if piece else near_x
            slot = 3 - target
        return pltpu.make_async_remote_copy(
            src_ref=chip_out.at[t, k, piece], dst_ref=chip_in.at[t, slot, piece],
            send_sem=chip_send.at[t, k, piece], recv_sem=chip_recv.at[t, slot, piece],
            device_id=(target * 2 + core, z), device_id_type=MESH)

    def chip_arrival(t, k, piece):
        return pltpu.make_async_remote_copy(
            src_ref=chip_in.at[t, k, piece], dst_ref=chip_in.at[t, k, piece],
            send_sem=chip_send.at[t, k, piece], recv_sem=chip_recv.at[t, k, piece],
            device_id=(sibling, z), device_id_type=MESH)

    def block(owner, t, piece=slice(None)):
        return grads[piece, pl.ds(pl.multiple_of(owner * rows, rows), rows), pl.ds(pl.multiple_of(t * tile, tile), tile)]

    def paired(t, k, piece):
        return block(k * 2 + core, t, piece) + sib_in[t, k, piece].astype(f32)

    def core_stage(t):
        for k in range(n_chip):
            sib_out[t, k] = block(k * 2 + (1 - core), t).astype(b16)
        sib_copy(t).start()

    def chip_stage(t):
        sib_copy(t).wait_recv()
        if square:
            sends = [(diagonal, 0), (diagonal, 1), (near_x, 0), (near_y, 1)]
        else:
            sends = [(k, piece) for k in direct for piece in range(2)]
        for k, piece in sends:
            chip_out[t, k, piece] = paired(t, k, piece).astype(b16)
            chip_copy(t, k, piece).start()

    def relay_stage(t):
        if square:
            for piece, k in enumerate((near_y, near_x)):
                chip_arrival(t, diagonal, piece).wait_recv()
                chip_out[t, k, piece] = (
                    paired(t, k, piece) + chip_in[t, diagonal, piece].astype(f32)
                ).astype(b16)
                chip_copy(t, k, piece).start()

    def send_own(piece):
        @pl.when(z < n_mp - 1)
        def _():
            tok_copy(z, piece, 0, z + 1).start()

        @pl.when(z > 0)
        def _():
            tok_copy(z, piece, 1, z - 1).start()

    held[z, 1] = cot_ref[...]
    own_rows = pl.ds(pl.multiple_of(dp * rows, rows), rows)
    weights[0, own_rows, :] = win_ref[...].astype(b16)
    weights[1, own_rows, :] = wout_ref[...].T.astype(b16)
    pl.semaphore_wait(barrier, n_chip + n_mp - 1)
    send_own(1)
    for piece in range(2):
        for k in direct:
            weight_copy(dp, piece, w_send.at[k, piece], k * 2 + core).start()
        weight_copy(dp, piece, w_sib.at[chip, piece], sibling).start()
    values = tokens_ref[...].astype(f32)
    inverse = lax.rsqrt(jnp.mean(values * values, axis=-1, keepdims=True) + 1e-06)
    held[z, 0] = (values * inverse).astype(b16)
    send_own(0)

    def clear(i, carry):
        part = pl.ds(pl.multiple_of(i * rows, rows), rows)
        grads[:, part, :] = jnp.zeros((2, rows, hidden_units), f32)
        return carry

    lax.fori_loop(0, n_dp, clear, 0)

    for k, piece, relay in arrivals:
        weight_copy(k * 2 + core, piece, w_sib.at[k, piece], sibling).wait_recv()
        if relay is not None:
            weight_copy(k * 2 + core, piece, w_relay.at[piece], relay * 2 + core).start()
        weight_copy(k * 2 + core, piece, w_sib.at[k, piece], sibling).start()

    def pass_on(distance):
        for piece in (1, 0):
            @pl.when(z - distance >= 0)
            def _():
                tok_copy(z - distance, piece, 0, z).wait_recv()

                @pl.when(z < n_mp - 1)
                def _():
                    tok_copy(z - distance, piece, 0, z + 1).start()

            @pl.when(z + distance < n_mp)
            def _():
                tok_copy(z + distance, piece, 1, z).wait_recv()

                @pl.when(z > 0)
                def _():
                    tok_copy(z + distance, piece, 1, z - 1).start()

    at_end = (z == 0) | (z == n_mp - 1)

    pass_on(1)
    for k in range(n_chip):
        for piece in range(2):
            weight_copy(k * 2 + (1 - core), piece, w_sib.at[k, piece], sibling).wait_recv()

    furthest = jnp.where(z > n_mp - 1 - z, z, n_mp - 1 - z)

    def chunk(origin, last):
        flipped[0] = held[origin, 0].T
        flipped[1] = held[origin, 1].T

        def columns(step, carry):
            part = pl.ds(pl.multiple_of(step * tile, tile), tile)
            w_in = weights[0, :, part]
            preact = jnp.dot(held[origin, 0], w_in, preferred_element_type=f32)
            d_hidden = jnp.dot(held[origin, 1], weights[1, :, part], preferred_element_type=f32)
            hidden, slope = gelu_pair(preact)
            d_preact = (d_hidden * slope).astype(b16)
            grads[0, :, part] += jnp.dot(flipped[0], d_preact, preferred_element_type=f32)
            grads[1, :, part] += jnp.dot(flipped[1], hidden.astype(b16), preferred_element_type=f32)
            back = lax.dot_general(d_preact, w_in, (((1,), (1,)), ((), ())), preferred_element_type=f32)

            @pl.when(step == 0)
            def _():
                dn[...] = back

            @pl.when(step > 0)
            def _():
                dn[...] += back

            @pl.when(last)
            def _():
                core_stage(step)

                @pl.when(step > 0)
                def _():
                    chip_stage(step - 1)

                @pl.when(step > 1)
                def _():
                    relay_stage(step - 2)
            return carry

        lax.fori_loop(0, n_tile, columns, 0)

        @pl.when(origin == z)
        def _():
            own[...] = dn[...]

        @pl.when(origin != z)
        def _():
            ret_out[origin] = dn[...].astype(b16)

            @pl.when(at_end)
            def _():
                for step in range(n_ret):
                    ret_copy(origin, step, jnp.where(z == 0, 1, -1)).start()

    def at_distance(distance, carry):
        def side(which, inner):
            ahead = distance + which

            @pl.when((ahead >= 2) & (ahead < n_mp) & (which == jnp.where(at_end, 0, 1)))
            def _():
                pass_on(ahead)

            origin = z + distance * (2 * which - 1)

            @pl.when((origin >= 0) & (origin < n_mp) & (distance + which > 0))
            def _():
                chunk(origin, (distance == furthest) & ((which == 1) | (z + distance >= n_mp)))
            return inner

        lax.fori_loop(jnp.where(distance == 0, 1, 0), 2, side, 0)
        return carry

    lax.fori_loop(0, n_mp, at_distance, 0)

    chip_stage(n_tile - 1)
    for t in range(max(0, n_tile - 2), n_tile):
        relay_stage(t)

    def hand_on(far, carry):
        for step in range(n_ret):
            for turn in range(2):
                down = (turn + z // (n_mp // 2)) % 2
                way = 1 - 2 * down
                target = far + down * (n_mp - 1 - 2 * far)

                @pl.when(((target - z) * way > 0) & jnp.logical_not(at_end))
                def _():
                    part = pl.ds(step * ret_rows, ret_rows)
                    ret_arrival(target, step).wait_recv()
                    ret_out[target, part] = (
                        ret_out[target, part].astype(f32) + ret_in[target, part].astype(f32)
                    ).astype(b16)
                    ret_copy(target, step, way).start()
        return carry

    lax.fori_loop(1, n_mp, hand_on, 0)

    for t in range(n_tile):
        totals = []
        for piece in range(2):
            total = paired(t, chip, piece)
            for k in direct:
                chip_arrival(t, k, piece).wait_recv()
                total += chip_in[t, k, piece].astype(f32)
            totals.append(total)
        gin_ref[:, t * tile:(t + 1) * tile] = totals[0]
        gout_ref[t * tile:(t + 1) * tile, :] = totals[1].T

    @pl.when(z < n_mp - 1)
    def _():
        for step in range(n_ret):
            ret_arrival(z, step).wait_recv()
        own[...] += ret_in[z].astype(f32)

    @pl.when(z > 0)
    def _():
        for step in range(n_ret):
            ret_arrival(n_mp, step).wait_recv()
        own[...] += ret_in[n_mp].astype(f32)

    values = tokens_ref[...].astype(f32)
    inverse = lax.rsqrt(jnp.mean(values * values, axis=-1, keepdims=True) + 1e-06)
    normed = values * inverse
    d_normed = own[...]
    d_rows = inverse * (d_normed - normed * jnp.mean(d_normed * normed, axis=-1, keepdims=True))
    ig_ref[...] = d_rows.astype(b16)

    for piece in range(2):
        for k in direct:
            weight_copy(dp, piece, w_send.at[k, piece], k * 2 + core).wait_send()
        for k, arrived, relay in arrivals:
            if relay is not None and arrived == piece:
                weight_copy(k * 2 + core, piece, w_relay.at[piece], relay * 2 + core).wait_send()
        for t in range(n_tile):
            for k in direct + [diagonal] * square:
                chip_copy(t, k, piece).wait_send()
        for k in range(n_chip):
            weight_copy(k * 2 + core, piece, w_sib.at[k, piece], sibling).wait_send()
    for t in range(n_tile):
        sib_copy(t).wait_send()
    for origin in range(n_mp):
        for piece in range(2):
            @pl.when((z < n_mp - 1) & (origin <= z))
            def _():
                tok_copy(origin, piece, 0, z + 1).wait_send()

            @pl.when((z > 0) & (origin >= z))
            def _():
                tok_copy(origin, piece, 1, z - 1).wait_send()
    for i in range(1, n_mp):
        target = (z + i) % n_mp
        for step in range(n_ret):
            ret_copy(target, step, jnp.where(target > z, 1, -1)).wait_send()


def shards(n_dp, n_mp, tokens, cotangent, weight_in, weight_out, moment_in, second_in, moment_out, second_out):
    count, width = tokens.shape
    rows, units = weight_in.shape
    n_chip = n_dp // 2
    n_ret = 4
    tile = min(256, units)
    n_tile = units // tile
    b16, f32 = jnp.bfloat16, jnp.float32
    vmem = pl.BlockSpec(memory_space=pltpu.VMEM)
    dma = pltpu.SemaphoreType.DMA
    flops = 10 * count * n_mp * width * units
    input_grad, grad_in, grad_out = pl.pallas_call(
        functools.partial(kernel, n_dp, n_mp, tile),
        out_shape=(
            jax.ShapeDtypeStruct((count, width), b16),
            jax.ShapeDtypeStruct((rows, units), f32),
            jax.ShapeDtypeStruct((units, rows), f32),
        ),
        in_specs=[vmem] * 4,
        out_specs=(vmem,) * 3,
        scratch_shapes=[
            pltpu.VMEM((n_mp, 2, count, width), b16),
            pltpu.VMEM((2, width, units), b16),
            pltpu.VMEM((2, width, units), f32),
            pltpu.VMEM((2, width, count), b16),
            pltpu.VMEM((count, width), f32),
            pltpu.VMEM((count, width), f32),
            pltpu.VMEM((n_mp, count, width), b16),
            pltpu.VMEM((n_mp + 1, count, width), b16),
            pltpu.VMEM((n_tile, n_chip, 2, rows, tile), b16),
            pltpu.VMEM((n_tile, n_chip, 2, rows, tile), b16),
            pltpu.VMEM((n_tile, n_chip, 2, rows, tile), b16),
            pltpu.VMEM((n_tile, n_chip, 2, rows, tile), b16),
            dma((2, n_mp, 2)), dma((n_mp, 2)),
            dma((n_chip, 2)), dma((2,)), dma((n_chip, 2)), dma((n_dp, 2)),
            dma((n_mp, n_ret)), dma((n_mp + 1, n_ret)),
            dma((n_tile,)), dma((n_tile,)),
            dma((n_tile, n_chip, 2)), dma((n_tile, n_chip, 2)),
        ],
        compiler_params=pltpu.CompilerParams(
            collective_id=0, has_side_effects=True, vmem_limit_bytes=56 * 1024 * 1024
        ),
        cost_estimate=pl.CostEstimate(flops=flops, bytes_accessed=8 * rows * units * 4, transcendentals=0),
    )(tokens, cotangent, weight_in, weight_out)
    grad_scale = 1.0 / jnp.sqrt(jnp.float32(count * n_dp * n_mp))
    new_in = adam_step(weight_in, moment_in, second_in, grad_in * grad_scale)
    new_out = adam_step(weight_out, moment_out, second_out, grad_out * grad_scale)
    return (input_grad, *new_in, *new_out)


def solution(mesh):
    return jax.shard_map(
        functools.partial(shards, mesh.shape["dp"], mesh.shape["mp"]),
        mesh=mesh,
        in_specs=(
            P(("dp", "mp"), None),
            P(("dp", "mp"), None),
            P("dp", "mp"),
            P("mp", "dp"),
            P("dp", "mp"),
            P("dp", "mp"),
            P("mp", "dp"),
            P("mp", "dp"),
        ),
        out_specs=(
            P(("dp", "mp"), None),
            P("dp", "mp"),
            P("dp", "mp"),
            P("dp", "mp"),
            P("mp", "dp"),
            P("mp", "dp"),
            P("mp", "dp"),
        ),
        check_vma=False,
    )
```

```python
import functools
import math

import jax
import jax.numpy as jnp
from jax import lax
from jax.experimental import pallas as pl
from jax.experimental.pallas import tpu as pltpu
from jax.sharding import PartitionSpec as P

MESH = pl.DeviceIdType.MESH
STEP = 1000

BETA_ONE = 0.9
BETA_TWO = 0.999
EPSILON = 1e-08
LEARN_RATE = 0.001
DECAY_RATE = 0.1
CUBIC = 0.044715
ROOT = math.sqrt(2.0 / math.pi)


def adam_step(weight, moment, second, gradient):
    moment_new = BETA_ONE * moment + (1.0 - BETA_ONE) * gradient
    second_new = BETA_TWO * second + (1.0 - BETA_TWO) * gradient * gradient
    first_fix = 1.0 - BETA_ONE ** float(STEP)
    second_fix = 1.0 - BETA_TWO ** float(STEP)
    update = moment_new / first_fix / (jnp.sqrt(second_new / second_fix) + EPSILON)
    weight_new = weight - LEARN_RATE * (update + DECAY_RATE * weight)
    return (weight_new, moment_new, second_new)


def gelu_pair(v):
    square = v * v
    t = jnp.tanh(ROOT * (v + CUBIC * (square * v)))
    half = 0.5 * (1.0 + t)
    slope = half + (0.5 * ROOT) * v * (1.0 - t * t) * (1.0 + (3.0 * CUBIC) * square)
    return v * half, slope


def kernel(
    n_dp, n_mp, tile,
    tokens_ref, cot_ref, win_ref, wout_ref,
    ig_ref, gin_ref, gout_ref,
    held, weights, grads, flipped, acts, dn, own, ret_out, ret_in, sib_out, sib_in, chip_out, chip_in,
    tok_send, tok_recv, w_send, w_sib, w_recv, ret_send, ret_recv, sib_send, sib_recv, chip_send, chip_recv,
):
    n_chip = n_dp // 2
    dp, z = lax.axis_index("dp"), lax.axis_index("mp")
    chip, core = dp // 2, dp % 2
    sibling = chip * 2 + (1 - core)
    rows = win_ref.shape[0]
    hidden_units = win_ref.shape[1]
    f32, b16 = jnp.float32, jnp.bfloat16
    n_tile = hidden_units // tile
    n_ret = ret_send.shape[1]
    ret_rows = tokens_ref.shape[0] // n_ret

    def other_chip(i):
        return (chip + i) % n_chip

    barrier = pltpu.get_barrier_semaphore()
    pl.semaphore_signal(barrier, inc=1, device_id=(sibling, z), device_id_type=MESH)
    for i in range(1, n_chip):
        pl.semaphore_signal(barrier, inc=1, device_id=(other_chip(i) * 2 + core, z), device_id_type=MESH)
    for i in range(1, n_mp):
        pl.semaphore_signal(barrier, inc=1, device_id=(dp, (z + i) % n_mp), device_id_type=MESH)

    values = tokens_ref[...].astype(f32)
    inverse = lax.rsqrt(jnp.mean(values * values, axis=-1, keepdims=True) + 1e-06)
    held[z, 0] = (values * inverse).astype(b16)
    held[z, 1] = cot_ref[...]
    own_rows = pl.ds(pl.multiple_of(dp * rows, rows), rows)
    weights[0, own_rows, :] = win_ref[...].astype(b16)
    weights[1, own_rows, :] = wout_ref[...].T.astype(b16)
    pl.semaphore_wait(barrier, n_chip + n_mp - 1)

    def tok_copy(origin, piece, side, target):
        return pltpu.make_async_remote_copy(
            src_ref=held.at[origin, piece], dst_ref=held.at[origin, piece],
            send_sem=tok_send.at[side, origin, piece], recv_sem=tok_recv.at[origin, piece],
            device_id=(dp, target), device_id_type=MESH)

    def weight_copy(owner, send_sem, target):
        block = weights.at[:, pl.ds(pl.multiple_of(owner * rows, rows), rows), :]
        return pltpu.make_async_remote_copy(
            src_ref=block, dst_ref=block, send_sem=send_sem, recv_sem=w_recv.at[owner],
            device_id=(target, z), device_id_type=MESH)

    def ret_copy(target, step, way):
        part = pl.ds(step * ret_rows, ret_rows)
        slot = jnp.where((z + way == target) & (way == 1), n_mp, target)
        return pltpu.make_async_remote_copy(
            src_ref=ret_out.at[target, part], dst_ref=ret_in.at[slot, part],
            send_sem=ret_send.at[target, step], recv_sem=ret_recv.at[slot, step],
            device_id=(dp, z + way), device_id_type=MESH)

    def ret_arrival(slot, step):
        part = pl.ds(step * ret_rows, ret_rows)
        return pltpu.make_async_remote_copy(
            src_ref=ret_in.at[slot, part], dst_ref=ret_in.at[slot, part],
            send_sem=ret_send.at[0, step], recv_sem=ret_recv.at[slot, step],
            device_id=(dp, z), device_id_type=MESH)

    def sib_copy(t):
        return pltpu.make_async_remote_copy(
            src_ref=sib_out.at[t], dst_ref=sib_in.at[t],
            send_sem=sib_send.at[t], recv_sem=sib_recv.at[t],
            device_id=(sibling, z), device_id_type=MESH)

    def chip_copy(t, k):
        return pltpu.make_async_remote_copy(
            src_ref=chip_out.at[t, k], dst_ref=chip_in.at[t, chip],
            send_sem=chip_send.at[t, k], recv_sem=chip_recv.at[t, chip],
            device_id=(k * 2 + core, z), device_id_type=MESH)

    def chip_arrival(t, k):
        return pltpu.make_async_remote_copy(
            src_ref=chip_in.at[t, k], dst_ref=chip_in.at[t, k],
            send_sem=chip_send.at[t, k], recv_sem=chip_recv.at[t, k],
            device_id=(k * 2 + core, z), device_id_type=MESH)

    def block(owner, t):
        return grads[:, pl.ds(pl.multiple_of(owner * rows, rows), rows), pl.ds(pl.multiple_of(t * tile, tile), tile)]

    def core_stage(t):
        for k in range(n_chip):
            sib_out[t, k] = block(k * 2 + (1 - core), t).astype(b16)
        sib_copy(t).start()

    def chip_stage(t):
        sib_copy(t).wait_recv()
        for i in range(1, n_chip):
            k = other_chip(i)
            chip_out[t, k] = (block(k * 2 + core, t) + sib_in[t, k].astype(f32)).astype(b16)
            chip_copy(t, k).start()

    @pl.when(z < n_mp - 1)
    def _():
        for piece in range(2):
            tok_copy(z, piece, 0, z + 1).start()

    @pl.when(z > 0)
    def _():
        for piece in range(2):
            tok_copy(z, piece, 1, z - 1).start()

    for i in range(1, n_chip):
        k = other_chip(i)
        weight_copy(dp, w_send.at[k], k * 2 + core).start()
    weight_copy(dp, w_sib.at[chip], sibling).start()

    def clear(i, carry):
        part = pl.ds(pl.multiple_of(i * rows, rows), rows)
        grads[:, part, :] = jnp.zeros((2, rows, hidden_units), f32)
        return carry

    lax.fori_loop(0, n_dp, clear, 0)

    for i in range(1, n_chip):
        owner = other_chip(i) * 2 + core
        weight_copy(owner, w_sib.at[other_chip(i)], sibling).wait_recv()
        weight_copy(owner, w_sib.at[other_chip(i)], sibling).start()

    def pass_on(distance):
        for piece in range(2):
            @pl.when(z - distance >= 0)
            def _():
                tok_copy(z - distance, piece, 0, z).wait_recv()

                @pl.when(z < n_mp - 1)
                def _():
                    tok_copy(z - distance, piece, 0, z + 1).start()

            @pl.when(z + distance < n_mp)
            def _():
                tok_copy(z + distance, piece, 1, z).wait_recv()

                @pl.when(z > 0)
                def _():
                    tok_copy(z + distance, piece, 1, z - 1).start()

    pass_on(1)
    for k in range(n_chip):
        weight_copy(k * 2 + (1 - core), w_sib.at[k], sibling).wait_recv()

    furthest = jnp.where(z > n_mp - 1 - z, z, n_mp - 1 - z)
    at_end = (z == 0) | (z == n_mp - 1)

    def chunk(origin, last):
        def columns(step, carry):
            part = pl.ds(pl.multiple_of(step * tile, tile), tile)
            w_in = weights[0, :, part]
            preact = jnp.dot(held[origin, 0], w_in, preferred_element_type=f32)
            d_hidden = jnp.dot(held[origin, 1], weights[1, :, part], preferred_element_type=f32)
            hidden, slope = gelu_pair(preact)
            d_preact = (d_hidden * slope).astype(b16)
            acts[0, :, part] = d_preact
            acts[1, :, part] = hidden.astype(b16)
            back = lax.dot_general(d_preact, w_in, (((1,), (1,)), ((), ())), preferred_element_type=f32)

            @pl.when(step == 0)
            def _():
                dn[...] = back

            @pl.when(step > 0)
            def _():
                dn[...] += back
            return carry

        lax.fori_loop(0, n_tile, columns, 0)

        @pl.when(origin == z)
        def _():
            own[...] = dn[...]

        @pl.when(origin != z)
        def _():
            ret_out[origin] = dn[...].astype(b16)

            @pl.when(at_end)
            def _():
                for step in range(n_ret):
                    ret_copy(origin, step, jnp.where(z == 0, 1, -1)).start()

        flipped[0] = held[origin, 0].T
        flipped[1] = held[origin, 1].T

        def gradients(step, carry):
            part = pl.ds(pl.multiple_of(step * tile, tile), tile)
            for piece in range(2):
                grads[piece, :, part] += jnp.dot(flipped[piece], acts[piece, :, part], preferred_element_type=f32)

            @pl.when(last)
            def _():
                core_stage(step)

                @pl.when(step > 0)
                def _():
                    chip_stage(step - 1)
            return carry

        lax.fori_loop(0, n_tile, gradients, 0)

    def at_distance(distance, carry):
        @pl.when(distance >= 2)
        def _():
            pass_on(distance)

        def side(which, inner):
            origin = z + distance * (2 * which - 1)

            @pl.when((origin >= 0) & (origin < n_mp) & (distance + which > 0))
            def _():
                chunk(origin, (distance == furthest) & ((which == 1) | (z + distance >= n_mp)))
            return inner

        lax.fori_loop(jnp.where(distance == 0, 1, 0), 2, side, 0)
        return carry

    lax.fori_loop(0, n_mp, at_distance, 0)

    chip_stage(n_tile - 1)

    def hand_on(far, carry):
        for beat in range(n_ret + 1):
            for turn in range(2):
                step = beat - turn
                if not 0 <= step < n_ret:
                    continue
                down = (turn + z // (n_mp // 2)) % 2
                way = 1 - 2 * down
                target = far + down * (n_mp - 1 - 2 * far)

                @pl.when(((target - z) * way > 0) & jnp.logical_not(at_end))
                def _(step=step, way=way, target=target):
                    part = pl.ds(step * ret_rows, ret_rows)
                    ret_arrival(target, step).wait_recv()
                    ret_out[target, part] = (
                        ret_out[target, part].astype(f32) + ret_in[target, part].astype(f32)
                    ).astype(b16)
                    ret_copy(target, step, way).start()
        return carry

    lax.fori_loop(1, n_mp, hand_on, 0)

    for t in range(n_tile):
        total = block(dp, t) + sib_in[t, chip].astype(f32)
        for i in range(1, n_chip):
            k = other_chip(i)
            chip_arrival(t, k).wait_recv()
            total += chip_in[t, k].astype(f32)
        gin_ref[:, t * tile:(t + 1) * tile] = total[0]
        gout_ref[t * tile:(t + 1) * tile, :] = total[1].T

    @pl.when(z < n_mp - 1)
    def _():
        for step in range(n_ret):
            ret_arrival(z, step).wait_recv()
        own[...] += ret_in[z].astype(f32)

    @pl.when(z > 0)
    def _():
        for step in range(n_ret):
            ret_arrival(n_mp, step).wait_recv()
        own[...] += ret_in[n_mp].astype(f32)

    values = tokens_ref[...].astype(f32)
    inverse = lax.rsqrt(jnp.mean(values * values, axis=-1, keepdims=True) + 1e-06)
    normed = values * inverse
    d_normed = own[...]
    d_rows = inverse * (d_normed - normed * jnp.mean(d_normed * normed, axis=-1, keepdims=True))
    ig_ref[...] = d_rows.astype(b16)

    for i in range(1, n_chip):
        k = other_chip(i)
        weight_copy(dp, w_send.at[k], k * 2 + core).wait_send()
        for t in range(n_tile):
            chip_copy(t, k).wait_send()
    for k in range(n_chip):
        weight_copy(k * 2 + core, w_sib.at[k], sibling).wait_send()
    for t in range(n_tile):
        sib_copy(t).wait_send()
    for origin in range(n_mp):
        for piece in range(2):
            @pl.when((z < n_mp - 1) & (origin <= z))
            def _():
                tok_copy(origin, piece, 0, z + 1).wait_send()

            @pl.when((z > 0) & (origin >= z))
            def _():
                tok_copy(origin, piece, 1, z - 1).wait_send()
    for i in range(1, n_mp):
        target = (z + i) % n_mp
        for step in range(n_ret):
            ret_copy(target, step, jnp.where(target > z, 1, -1)).wait_send()


def shards(n_dp, n_mp, tokens, cotangent, weight_in, weight_out, moment_in, second_in, moment_out, second_out):
    count, width = tokens.shape
    rows, units = weight_in.shape
    n_chip = n_dp // 2
    n_ret = 4
    tile = min(256, units)
    n_tile = units // tile
    b16, f32 = jnp.bfloat16, jnp.float32
    vmem = pl.BlockSpec(memory_space=pltpu.VMEM)
    dma = pltpu.SemaphoreType.DMA
    flops = 10 * count * n_mp * width * units
    input_grad, grad_in, grad_out = pl.pallas_call(
        functools.partial(kernel, n_dp, n_mp, tile),
        out_shape=(
            jax.ShapeDtypeStruct((count, width), b16),
            jax.ShapeDtypeStruct((rows, units), f32),
            jax.ShapeDtypeStruct((units, rows), f32),
        ),
        in_specs=[vmem] * 4,
        out_specs=(vmem,) * 3,
        scratch_shapes=[
            pltpu.VMEM((n_mp, 2, count, width), b16),
            pltpu.VMEM((2, width, units), b16),
            pltpu.VMEM((2, width, units), f32),
            pltpu.VMEM((2, width, count), b16),
            pltpu.VMEM((2, count, units), b16),
            pltpu.VMEM((count, width), f32),
            pltpu.VMEM((count, width), f32),
            pltpu.VMEM((n_mp, count, width), b16),
            pltpu.VMEM((n_mp + 1, count, width), b16),
            pltpu.VMEM((n_tile, n_chip, 2, rows, tile), b16),
            pltpu.VMEM((n_tile, n_chip, 2, rows, tile), b16),
            pltpu.VMEM((n_tile, n_chip, 2, rows, tile), b16),
            pltpu.VMEM((n_tile, n_chip, 2, rows, tile), b16),
            dma((2, n_mp, 2)), dma((n_mp, 2)),
            dma((n_chip,)), dma((n_chip,)), dma((n_dp,)),
            dma((n_mp, n_ret)), dma((n_mp + 1, n_ret)),
            dma((n_tile,)), dma((n_tile,)),
            dma((n_tile, n_chip)), dma((n_tile, n_chip)),
        ],
        compiler_params=pltpu.CompilerParams(
            collective_id=0, has_side_effects=True, vmem_limit_bytes=56 * 1024 * 1024
        ),
        cost_estimate=pl.CostEstimate(flops=flops, bytes_accessed=8 * rows * units * 4, transcendentals=0),
    )(tokens, cotangent, weight_in, weight_out)
    grad_scale = 1.0 / jnp.sqrt(jnp.float32(count * n_dp * n_mp))
    new_in = adam_step(weight_in, moment_in, second_in, grad_in * grad_scale)
    new_out = adam_step(weight_out, moment_out, second_out, grad_out * grad_scale)
    return (input_grad, *new_in, *new_out)


def solution(mesh):
    return jax.shard_map(
        functools.partial(shards, mesh.shape["dp"], mesh.shape["mp"]),
        mesh=mesh,
        in_specs=(
            P(("dp", "mp"), None),
            P(("dp", "mp"), None),
            P("dp", "mp"),
            P("mp", "dp"),
            P("dp", "mp"),
            P("dp", "mp"),
            P("mp", "dp"),
            P("mp", "dp"),
        ),
        out_specs=(
            P(("dp", "mp"), None),
            P("dp", "mp"),
            P("dp", "mp"),
            P("dp", "mp"),
            P("mp", "dp"),
            P("mp", "dp"),
            P("mp", "dp"),
        ),
        check_vma=False,
    )
```

```python
import functools
import math

import jax
import jax.numpy as jnp
from jax import lax
from jax.experimental import pallas as pl
from jax.experimental.pallas import tpu as pltpu
from jax.sharding import PartitionSpec as P

MESH = pl.DeviceIdType.MESH
STEP = 1000

BETA_ONE = 0.9
BETA_TWO = 0.999
EPSILON = 1e-08
LEARN_RATE = 0.001
DECAY_RATE = 0.1
CUBIC = 0.044715
ROOT = math.sqrt(2.0 / math.pi)


def adam_step(weight, moment, second, gradient):
    moment_new = BETA_ONE * moment + (1.0 - BETA_ONE) * gradient
    second_new = BETA_TWO * second + (1.0 - BETA_TWO) * gradient * gradient
    first_fix = 1.0 - BETA_ONE ** float(STEP)
    second_fix = 1.0 - BETA_TWO ** float(STEP)
    update = moment_new / first_fix / (jnp.sqrt(second_new / second_fix) + EPSILON)
    weight_new = weight - LEARN_RATE * (update + DECAY_RATE * weight)
    return (weight_new, moment_new, second_new)


def gelu_pair(v):
    square = v * v
    t = jnp.tanh(ROOT * (v + CUBIC * (square * v)))
    half = 0.5 * (1.0 + t)
    slope = half + (0.5 * ROOT) * v * (1.0 - t * t) * (1.0 + (3.0 * CUBIC) * square)
    return v * half, slope


def kernel(
    n_dp, n_mp, tile,
    tokens_ref, cot_ref, win_ref, wout_ref,
    ig_ref, gin_ref, gout_ref,
    held, weights, grads, flipped, acts, dn, own, ret_out, ret_in, sib_out, sib_in, chip_out, chip_in,
    tok_send, tok_recv, w_send, w_relay, w_sib, w_recv, ret_send, ret_recv, sib_send, sib_recv, chip_send, chip_recv,
):
    n_chip = n_dp // 2
    dp, z = lax.axis_index("dp"), lax.axis_index("mp")
    chip, core = dp // 2, dp % 2
    sibling = chip * 2 + (1 - core)
    rows = win_ref.shape[0]
    hidden_units = win_ref.shape[1]
    f32, b16 = jnp.float32, jnp.bfloat16
    n_tile = hidden_units // tile
    n_ret = ret_send.shape[1]
    ret_rows = tokens_ref.shape[0] // n_ret

    def other_chip(i):
        return (chip + i) % n_chip

    barrier = pltpu.get_barrier_semaphore()
    pl.semaphore_signal(barrier, inc=1, device_id=(sibling, z), device_id_type=MESH)
    for i in range(1, n_chip):
        pl.semaphore_signal(barrier, inc=1, device_id=(other_chip(i) * 2 + core, z), device_id_type=MESH)
    for i in range(1, n_mp):
        pl.semaphore_signal(barrier, inc=1, device_id=(dp, (z + i) % n_mp), device_id_type=MESH)

    values = tokens_ref[...].astype(f32)
    inverse = lax.rsqrt(jnp.mean(values * values, axis=-1, keepdims=True) + 1e-06)
    held[z, 0] = (values * inverse).astype(b16)
    held[z, 1] = cot_ref[...]
    own_rows = pl.ds(pl.multiple_of(dp * rows, rows), rows)
    weights[0, own_rows, :] = win_ref[...].astype(b16)
    weights[1, own_rows, :] = wout_ref[...].T.astype(b16)
    pl.semaphore_wait(barrier, n_chip + n_mp - 1)

    def tok_copy(origin, piece, side, target):
        return pltpu.make_async_remote_copy(
            src_ref=held.at[origin, piece], dst_ref=held.at[origin, piece],
            send_sem=tok_send.at[side, origin, piece], recv_sem=tok_recv.at[origin, piece],
            device_id=(dp, target), device_id_type=MESH)

    def weight_copy(owner, piece, send_sem, target):
        block = weights.at[piece, pl.ds(pl.multiple_of(owner * rows, rows), rows), :]
        return pltpu.make_async_remote_copy(
            src_ref=block, dst_ref=block, send_sem=send_sem, recv_sem=w_recv.at[owner, piece],
            device_id=(target, z), device_id_type=MESH)

    square = n_chip == 4
    near_x, near_y, diagonal = chip + 1 - 2 * (chip % 2), (chip + 2) % 4, 3 - chip
    if square:
        direct = [near_x, near_y]
        arrivals = [
            (near_x, 0, near_y), (near_y, 1, near_x), (near_x, 1, None),
            (near_y, 0, None), (diagonal, 0, None), (diagonal, 1, None),
        ]
    else:
        direct = [other_chip(i) for i in range(1, n_chip)]
        arrivals = [(k, piece, None) for k in direct for piece in range(2)]

    def ret_copy(target, step, way):
        part = pl.ds(step * ret_rows, ret_rows)
        slot = jnp.where((z + way == target) & (way == 1), n_mp, target)
        return pltpu.make_async_remote_copy(
            src_ref=ret_out.at[target, part], dst_ref=ret_in.at[slot, part],
            send_sem=ret_send.at[target, step], recv_sem=ret_recv.at[slot, step],
            device_id=(dp, z + way), device_id_type=MESH)

    def ret_arrival(slot, step):
        part = pl.ds(step * ret_rows, ret_rows)
        return pltpu.make_async_remote_copy(
            src_ref=ret_in.at[slot, part], dst_ref=ret_in.at[slot, part],
            send_sem=ret_send.at[0, step], recv_sem=ret_recv.at[slot, step],
            device_id=(dp, z), device_id_type=MESH)

    def sib_copy(t):
        return pltpu.make_async_remote_copy(
            src_ref=sib_out.at[t], dst_ref=sib_in.at[t],
            send_sem=sib_send.at[t], recv_sem=sib_recv.at[t],
            device_id=(sibling, z), device_id_type=MESH)

    def chip_copy(t, k, piece):
        target, slot = k, chip
        if k is diagonal and square:
            target = near_y if piece else near_x
            slot = 3 - target
        return pltpu.make_async_remote_copy(
            src_ref=chip_out.at[t, k, piece], dst_ref=chip_in.at[t, slot, piece],
            send_sem=chip_send.at[t, k, piece], recv_sem=chip_recv.at[t, slot, piece],
            device_id=(target * 2 + core, z), device_id_type=MESH)

    def chip_arrival(t, k, piece):
        return pltpu.make_async_remote_copy(
            src_ref=chip_in.at[t, k, piece], dst_ref=chip_in.at[t, k, piece],
            send_sem=chip_send.at[t, k, piece], recv_sem=chip_recv.at[t, k, piece],
            device_id=(sibling, z), device_id_type=MESH)

    def block(owner, t, piece=slice(None)):
        return grads[piece, pl.ds(pl.multiple_of(owner * rows, rows), rows), pl.ds(pl.multiple_of(t * tile, tile), tile)]

    def paired(t, k, piece):
        return block(k * 2 + core, t, piece) + sib_in[t, k, piece].astype(f32)

    def core_stage(t):
        for k in range(n_chip):
            sib_out[t, k] = block(k * 2 + (1 - core), t).astype(b16)
        sib_copy(t).start()

    def chip_stage(t):
        sib_copy(t).wait_recv()
        if square:
            sends = [(diagonal, 0), (diagonal, 1), (near_x, 0), (near_y, 1)]
        else:
            sends = [(k, piece) for k in direct for piece in range(2)]
        for k, piece in sends:
            chip_out[t, k, piece] = paired(t, k, piece).astype(b16)
            chip_copy(t, k, piece).start()

    def relay_stage(t):
        if square:
            for piece, k in enumerate((near_y, near_x)):
                chip_arrival(t, diagonal, piece).wait_recv()
                chip_out[t, k, piece] = (
                    paired(t, k, piece) + chip_in[t, diagonal, piece].astype(f32)
                ).astype(b16)
                chip_copy(t, k, piece).start()

    @pl.when(z < n_mp - 1)
    def _():
        for piece in range(2):
            tok_copy(z, piece, 0, z + 1).start()

    @pl.when(z > 0)
    def _():
        for piece in range(2):
            tok_copy(z, piece, 1, z - 1).start()

    for piece in range(2):
        for k in direct:
            weight_copy(dp, piece, w_send.at[k, piece], k * 2 + core).start()
        weight_copy(dp, piece, w_sib.at[chip, piece], sibling).start()

    def clear(i, carry):
        part = pl.ds(pl.multiple_of(i * rows, rows), rows)
        grads[:, part, :] = jnp.zeros((2, rows, hidden_units), f32)
        return carry

    lax.fori_loop(0, n_dp, clear, 0)

    for k, piece, relay in arrivals:
        weight_copy(k * 2 + core, piece, w_sib.at[k, piece], sibling).wait_recv()
        if relay is not None:
            weight_copy(k * 2 + core, piece, w_relay.at[piece], relay * 2 + core).start()
        weight_copy(k * 2 + core, piece, w_sib.at[k, piece], sibling).start()

    def pass_on(distance):
        for piece in range(2):
            @pl.when(z - distance >= 0)
            def _():
                tok_copy(z - distance, piece, 0, z).wait_recv()

                @pl.when(z < n_mp - 1)
                def _():
                    tok_copy(z - distance, piece, 0, z + 1).start()

            @pl.when(z + distance < n_mp)
            def _():
                tok_copy(z + distance, piece, 1, z).wait_recv()

                @pl.when(z > 0)
                def _():
                    tok_copy(z + distance, piece, 1, z - 1).start()

    pass_on(1)
    for k in range(n_chip):
        for piece in range(2):
            weight_copy(k * 2 + (1 - core), piece, w_sib.at[k, piece], sibling).wait_recv()

    furthest = jnp.where(z > n_mp - 1 - z, z, n_mp - 1 - z)
    at_end = (z == 0) | (z == n_mp - 1)

    def chunk(origin, last):
        def columns(step, carry):
            part = pl.ds(pl.multiple_of(step * tile, tile), tile)
            w_in = weights[0, :, part]
            preact = jnp.dot(held[origin, 0], w_in, preferred_element_type=f32)
            d_hidden = jnp.dot(held[origin, 1], weights[1, :, part], preferred_element_type=f32)
            hidden, slope = gelu_pair(preact)
            d_preact = (d_hidden * slope).astype(b16)
            acts[0, :, part] = d_preact
            acts[1, :, part] = hidden.astype(b16)
            back = lax.dot_general(d_preact, w_in, (((1,), (1,)), ((), ())), preferred_element_type=f32)

            @pl.when(step == 0)
            def _():
                dn[...] = back

            @pl.when(step > 0)
            def _():
                dn[...] += back
            return carry

        lax.fori_loop(0, n_tile, columns, 0)

        @pl.when(origin == z)
        def _():
            own[...] = dn[...]

        @pl.when(origin != z)
        def _():
            ret_out[origin] = dn[...].astype(b16)

            @pl.when(at_end)
            def _():
                for step in range(n_ret):
                    ret_copy(origin, step, jnp.where(z == 0, 1, -1)).start()

        flipped[0] = held[origin, 0].T
        flipped[1] = held[origin, 1].T

        def gradients(step, carry):
            part = pl.ds(pl.multiple_of(step * tile, tile), tile)
            for piece in range(2):
                grads[piece, :, part] += jnp.dot(flipped[piece], acts[piece, :, part], preferred_element_type=f32)

            @pl.when(last)
            def _():
                core_stage(step)

                @pl.when(step > 0)
                def _():
                    chip_stage(step - 1)
            return carry

        lax.fori_loop(0, n_tile, gradients, 0)

    def at_distance(distance, carry):
        @pl.when(distance >= 2)
        def _():
            pass_on(distance)

        def side(which, inner):
            origin = z + distance * (2 * which - 1)

            @pl.when((origin >= 0) & (origin < n_mp) & (distance + which > 0))
            def _():
                chunk(origin, (distance == furthest) & ((which == 1) | (z + distance >= n_mp)))
            return inner

        lax.fori_loop(jnp.where(distance == 0, 1, 0), 2, side, 0)
        return carry

    lax.fori_loop(0, n_mp, at_distance, 0)

    chip_stage(n_tile - 1)
    for t in range(n_tile):
        relay_stage(t)

    def hand_on(far, carry):
        for beat in range(n_ret + 1):
            for turn in range(2):
                step = beat - turn
                if not 0 <= step < n_ret:
                    continue
                down = (turn + z // (n_mp // 2)) % 2
                way = 1 - 2 * down
                target = far + down * (n_mp - 1 - 2 * far)

                @pl.when(((target - z) * way > 0) & jnp.logical_not(at_end))
                def _(step=step, way=way, target=target):
                    part = pl.ds(step * ret_rows, ret_rows)
                    ret_arrival(target, step).wait_recv()
                    ret_out[target, part] = (
                        ret_out[target, part].astype(f32) + ret_in[target, part].astype(f32)
                    ).astype(b16)
                    ret_copy(target, step, way).start()
        return carry

    lax.fori_loop(1, n_mp, hand_on, 0)

    for t in range(n_tile):
        totals = []
        for piece in range(2):
            total = paired(t, chip, piece)
            for k in direct:
                chip_arrival(t, k, piece).wait_recv()
                total += chip_in[t, k, piece].astype(f32)
            totals.append(total)
        gin_ref[:, t * tile:(t + 1) * tile] = totals[0]
        gout_ref[t * tile:(t + 1) * tile, :] = totals[1].T

    @pl.when(z < n_mp - 1)
    def _():
        for step in range(n_ret):
            ret_arrival(z, step).wait_recv()
        own[...] += ret_in[z].astype(f32)

    @pl.when(z > 0)
    def _():
        for step in range(n_ret):
            ret_arrival(n_mp, step).wait_recv()
        own[...] += ret_in[n_mp].astype(f32)

    values = tokens_ref[...].astype(f32)
    inverse = lax.rsqrt(jnp.mean(values * values, axis=-1, keepdims=True) + 1e-06)
    normed = values * inverse
    d_normed = own[...]
    d_rows = inverse * (d_normed - normed * jnp.mean(d_normed * normed, axis=-1, keepdims=True))
    ig_ref[...] = d_rows.astype(b16)

    for piece in range(2):
        for k in direct:
            weight_copy(dp, piece, w_send.at[k, piece], k * 2 + core).wait_send()
        for k, arrived, relay in arrivals:
            if relay is not None and arrived == piece:
                weight_copy(k * 2 + core, piece, w_relay.at[piece], relay * 2 + core).wait_send()
        for t in range(n_tile):
            for k in direct + [diagonal] * square:
                chip_copy(t, k, piece).wait_send()
        for k in range(n_chip):
            weight_copy(k * 2 + core, piece, w_sib.at[k, piece], sibling).wait_send()
    for t in range(n_tile):
        sib_copy(t).wait_send()
    for origin in range(n_mp):
        for piece in range(2):
            @pl.when((z < n_mp - 1) & (origin <= z))
            def _():
                tok_copy(origin, piece, 0, z + 1).wait_send()

            @pl.when((z > 0) & (origin >= z))
            def _():
                tok_copy(origin, piece, 1, z - 1).wait_send()
    for i in range(1, n_mp):
        target = (z + i) % n_mp
        for step in range(n_ret):
            ret_copy(target, step, jnp.where(target > z, 1, -1)).wait_send()


def shards(n_dp, n_mp, tokens, cotangent, weight_in, weight_out, moment_in, second_in, moment_out, second_out):
    count, width = tokens.shape
    rows, units = weight_in.shape
    n_chip = n_dp // 2
    n_ret = 4
    tile = min(256, units)
    n_tile = units // tile
    b16, f32 = jnp.bfloat16, jnp.float32
    vmem = pl.BlockSpec(memory_space=pltpu.VMEM)
    dma = pltpu.SemaphoreType.DMA
    flops = 10 * count * n_mp * width * units
    input_grad, grad_in, grad_out = pl.pallas_call(
        functools.partial(kernel, n_dp, n_mp, tile),
        out_shape=(
            jax.ShapeDtypeStruct((count, width), b16),
            jax.ShapeDtypeStruct((rows, units), f32),
            jax.ShapeDtypeStruct((units, rows), f32),
        ),
        in_specs=[vmem] * 4,
        out_specs=(vmem,) * 3,
        scratch_shapes=[
            pltpu.VMEM((n_mp, 2, count, width), b16),
            pltpu.VMEM((2, width, units), b16),
            pltpu.VMEM((2, width, units), f32),
            pltpu.VMEM((2, width, count), b16),
            pltpu.VMEM((2, count, units), b16),
            pltpu.VMEM((count, width), f32),
            pltpu.VMEM((count, width), f32),
            pltpu.VMEM((n_mp, count, width), b16),
            pltpu.VMEM((n_mp + 1, count, width), b16),
            pltpu.VMEM((n_tile, n_chip, 2, rows, tile), b16),
            pltpu.VMEM((n_tile, n_chip, 2, rows, tile), b16),
            pltpu.VMEM((n_tile, n_chip, 2, rows, tile), b16),
            pltpu.VMEM((n_tile, n_chip, 2, rows, tile), b16),
            dma((2, n_mp, 2)), dma((n_mp, 2)),
            dma((n_chip, 2)), dma((2,)), dma((n_chip, 2)), dma((n_dp, 2)),
            dma((n_mp, n_ret)), dma((n_mp + 1, n_ret)),
            dma((n_tile,)), dma((n_tile,)),
            dma((n_tile, n_chip, 2)), dma((n_tile, n_chip, 2)),
        ],
        compiler_params=pltpu.CompilerParams(
            collective_id=0, has_side_effects=True, vmem_limit_bytes=56 * 1024 * 1024
        ),
        cost_estimate=pl.CostEstimate(flops=flops, bytes_accessed=8 * rows * units * 4, transcendentals=0),
    )(tokens, cotangent, weight_in, weight_out)
    grad_scale = 1.0 / jnp.sqrt(jnp.float32(count * n_dp * n_mp))
    new_in = adam_step(weight_in, moment_in, second_in, grad_in * grad_scale)
    new_out = adam_step(weight_out, moment_out, second_out, grad_out * grad_scale)
    return (input_grad, *new_in, *new_out)


def solution(mesh):
    return jax.shard_map(
        functools.partial(shards, mesh.shape["dp"], mesh.shape["mp"]),
        mesh=mesh,
        in_specs=(
            P(("dp", "mp"), None),
            P(("dp", "mp"), None),
            P("dp", "mp"),
            P("mp", "dp"),
            P("dp", "mp"),
            P("dp", "mp"),
            P("mp", "dp"),
            P("mp", "dp"),
        ),
        out_specs=(
            P(("dp", "mp"), None),
            P("dp", "mp"),
            P("dp", "mp"),
            P("dp", "mp"),
            P("mp", "dp"),
            P("mp", "dp"),
            P("mp", "dp"),
        ),
        check_vma=False,
    )
```
